128 devices in a mesh: expert: 16 (over z_hi, x, core), fsdp: 8 (over z_lo, y).
Axes of the slice: x: 4, y: 4, z: 4 (z_hi: 2, z_lo: 2; z = z_hi * 2 + z_lo), core: 2. Of those that a mesh axis runs over, the one named last changes fastest.
Arguments:
- out_grad: bfloat16 [32768, 7168], P(('expert', 'fsdp')), may hold values from -6 to 6
- expert_ids: int32 [32768, 1], P(('expert', 'fsdp')), may hold values from 0 to 15; in each aligned block of 256 rows (0 to 255, 256 to 511, ...) at most 48 rows name the same one
- stash_codes: bfloat16 [16, 8, 16, 48, 2048], P('expert', 'fsdp'), may hold values from -4 to 4
- stash_scale: int32 [16, 8, 16, 48, 16], P('expert', 'fsdp'), may hold values from -2 to 1
- down_weight: bfloat16 [16, 1024, 7168], P('expert', None, 'fsdp'), may hold values from -0.1875 to 0.1875
Outputs:
- in_grad: bfloat16 [32768, 2048], P(('expert', 'fsdp'))
- weight_grad: bfloat16 [16, 1024, 7168], P('expert', None, 'fsdp')
The draws below stay inside these ranges and needn't reach their ends.
Inputs may be any that keep to these rules, and one draw needn't show every extreme that they name: `expert_ids`: among the 256 rows of one device, at most 48 name the same expert, and in every draw some device has an expert named by exactly 48 of its rows.
All inputs are finite; a program needn't handle non-finite values.
Results may differ from the reference program's by a relative error of at most 0.017.
Values may be sent and summed in bfloat16 or wider, within the bound.
A program may use at most 192 MiB of HBM per device.

```python
import math
import jax
import jax.numpy as jnp
import numpy as np
from jax import lax

D = 7168
FFW = 1024
BLOCK = 128
ROWS_DEV = 256
EXPERTS = 16
SOURCES = 16
REPLICAS = 8
CAP = 48
ROWS = 32768


def set_ends(values, own_key, least, high):
    dims = values.shape
    place = [jax.random.randint(jax.random.fold_in(own_key, axis), (), 0, dims[axis]) for axis in range(len(dims))]
    values = values.at[tuple(place)].set(least)
    longest = dims.index(max(dims))
    place[longest] = (place[longest] + 1) % dims[longest]
    return values.at[tuple(place)].set(high)


def shard_levels(rng, shape, shards, low, top_value):
    loudness = 1.0
    for dim, blocks in shards:
        heights = jax.random.uniform(jax.random.fold_in(jax.random.fold_in(rng, 6), dim), (blocks,), jnp.float32, low / len(shards), top_value / len(shards))
        loudness = loudness * jnp.repeat(jnp.exp(heights), shape[dim] // blocks).reshape((-1,) + (1,) * (len(shape) - 1 - dim))
    return loudness


def assign_block(rng, own, number, rows, number_of, top, limit, lean):
    ranking = jax.random.permutation(rng, number_of)
    packed, usual = load_shares(number_of, rows * top, limit, lean, True), load_shares(number_of, rows * top, limit, lean, False)
    places = jnp.arange(number_of)

    def named(tallies, rotation):
        used = int((tallies > 0).sum())
        fixed = max(1, used // 4)
        shifted = fixed + (places - fixed + rotation * (used - fixed)) % max(1, number_of - fixed)
        return jnp.zeros((number_of,), jnp.int32).at[ranking[jnp.where(places < fixed, places, shifted)]].set(jnp.asarray(tallies, jnp.int32))

    tallies = jnp.where(number % 4 == 0, named(packed, number // 4), named(usual, number - number // 4 - 1))
    mixed = jax.random.permutation(jax.random.fold_in(own, 3), number_of)
    source_of, sink = mixed[0:number_of // 2 * 2:2], mixed[1:number_of // 2 * 2:2]
    margin = jnp.minimum(tallies[source_of] - 1, limit - tallies[sink]) // 2
    margin = jnp.where((source_of == ranking[0]) | (sink == ranking[0]) | (tallies[sink] == 0), 0, jnp.maximum(margin, 0))
    shifted = jax.random.randint(jax.random.fold_in(own, 4), (number_of // 2,), 0, 1 << 20) % (margin + 1)
    tallies = tallies.at[source_of].add(-shifted).at[sink].add(shifted)
    labels = jnp.searchsorted(jnp.cumsum(tallies), jnp.arange(rows * top), side="right").astype(jnp.int32)
    listing = labels.reshape(top, rows).T
    listing = listing[jax.random.permutation(jax.random.fold_in(own, 1), rows)]
    rotation = jax.random.randint(jax.random.fold_in(own, 2), (rows, 1), 0, top)
    return jnp.take_along_axis(listing, (jnp.arange(top)[None, :] + rotation) % top, axis=1)


def load_shares(number_of, total, limit, lean, full):
    loads = [(1 << 20) // math.isqrt(rank ** lean) + 1 for rank in range(1, number_of + 1)]
    largest = limit if full else min(limit, max(-(-total // number_of), total * loads[0] // sum(loads)))
    least = 1 if total - largest >= number_of - 1 else 0
    holding, rest = [largest] + [least] * (number_of - 1), total - largest - least * (number_of - 1)
    while rest > 0:
        movable = [i for i in range(1, number_of) if holding[i] < largest] or [i for i in range(1, number_of) if holding[i] < limit]
        pool, remaining = sum([loads[i] for i in movable]), rest
        for i in movable:
            extra = min(limit - holding[i], max(1, remaining * loads[i] // pool), rest)
            holding[i] = holding[i] + extra
            rest = rest - extra
    return np.array(holding)


def centred(own_key, extent, scale, bound, shards=(), kind=jnp.bfloat16):
    array = jax.random.normal(own_key, extent, jnp.float32) * scale
    if len(shards) > 0:
        array = shard_levels(own_key, extent, shards, -0.22, 0.18) * array
    return jnp.clip(array, min=-bound, max=bound).astype(kind)


def setup_inputs(seed: int = 0) -> dict:
    keys = jax.random.split(jax.random.key(seed), 6)
    out_grad = centred(keys[0], (ROWS, D), 1.0, 6.0, ((0, 128),))
    expert_ids_keys = jax.random.split(jax.random.fold_in(keys[1], 1), ROWS // ROWS_DEV)
    expert_ids_turns = jax.random.permutation(jax.random.fold_in(keys[1], 3), ROWS // ROWS_DEV)
    expert_ids = jax.vmap(lambda own, number: assign_block(jax.random.fold_in(keys[1], 2), own, number, ROWS_DEV, EXPERTS, 1, CAP, 2))(expert_ids_keys, expert_ids_turns).reshape((ROWS, 1))
    stash_codes = centred(keys[2], (EXPERTS, REPLICAS, SOURCES, CAP, 2 * FFW), 1.0, 4.0, ((0, 16), (1, 8)))
    stash_scale = set_ends(jax.random.randint(keys[3], (EXPERTS, REPLICAS, SOURCES, CAP, 2 * FFW // BLOCK), -2, 2), jax.random.fold_in(keys[3], 1), -2, 1).astype(jnp.int32)
    down_weight = centred(keys[4], (EXPERTS, FFW, D), FFW ** -0.5, 0.1875, ((0, 16), (2, 8)))
    return dict(out_grad=out_grad, expert_ids=expert_ids, stash_codes=stash_codes, stash_scale=stash_scale, down_weight=down_weight)


def swiglu_back(stash_values, scale_values, grad_rows, weight):
    factor = jnp.repeat(jnp.exp2(scale_values.astype(jnp.float32)), BLOCK, axis=1)
    values = stash_values.astype(jnp.float32) * factor
    gate_value = values[:, :FFW]
    up_value = values[:, FFW:]
    sigmoid_gate = jax.nn.sigmoid(gate_value)
    silu_gate = gate_value * sigmoid_gate
    hidden = (silu_gate * up_value).astype(jnp.bfloat16)
    d_hidden = jnp.dot(grad_rows, weight.T, preferred_element_type=jnp.float32)
    d_up = d_hidden * silu_gate
    d_gate = d_hidden * up_value * sigmoid_gate * (1.0 + gate_value * (1.0 - sigmoid_gate))
    returned_rows = jnp.concatenate([d_gate, d_up], axis=1).astype(jnp.bfloat16)
    partial_value = jnp.dot(hidden.T, grad_rows, preferred_element_type=jnp.float32).astype(jnp.bfloat16)
    return returned_rows, partial_value


def reference(out_grad, expert_ids, stash_codes, stash_scale, down_weight):
    expert_of = expert_ids[:, 0].reshape(SOURCES, REPLICAS, ROWS_DEV)
    row_block = out_grad.reshape(SOURCES, REPLICAS, ROWS_DEV, D)
    onehot = (expert_of[..., None] == jnp.arange(EXPERTS, dtype=jnp.int32)).astype(jnp.int32)
    slot_of = jnp.sum((jnp.cumsum(onehot, axis=2) - onehot) * onehot, axis=3).astype(jnp.int32)
    source_index = jnp.broadcast_to(jnp.arange(SOURCES, dtype=jnp.int32)[:, None], (SOURCES, ROWS_DEV))

    def per_expert(expert):
        weight = down_weight[expert]

        def per_replica(running, replica):
            slot_index = jnp.where(expert_of[:, replica] == expert, slot_of[:, replica], CAP).astype(jnp.int32)
            buffer = jnp.zeros((SOURCES, CAP, D), out_grad.dtype)
            buffer = buffer.at[source_index, slot_index].set(row_block[:, replica], mode="drop")
            returned_rows, partial_value = swiglu_back(
                stash_codes[expert, replica].reshape(SOURCES * CAP, 2 * FFW),
                stash_scale[expert, replica].reshape(SOURCES * CAP, 2 * FFW // BLOCK),
                buffer.reshape(SOURCES * CAP, D),
                weight,
            )
            partial_value = lax.optimization_barrier(partial_value)
            return running + partial_value.astype(jnp.float32), returned_rows.reshape(SOURCES, CAP, 2 * FFW)

        running, gradient_slots = lax.scan(per_replica, jnp.zeros((FFW, D), jnp.float32), jnp.arange(REPLICAS, dtype=jnp.int32))
        return running.astype(jnp.bfloat16), gradient_slots

    weight_grads, gradient_slots = lax.map(per_expert, jnp.arange(EXPERTS, dtype=jnp.int32))
    replica_index = jnp.arange(REPLICAS, dtype=jnp.int32)[None, :, None]
    source_rows = jnp.arange(SOURCES, dtype=jnp.int32)[:, None, None]
    in_grad = gradient_slots[expert_of, replica_index, source_rows, slot_of]
    return in_grad.reshape(ROWS, 2 * FFW), weight_grads
```

```python
import jax
import jax.numpy as jnp
from jax import lax
from jax.experimental import pallas as pl
from jax.experimental.pallas import tpu as pltpu
from jax.sharding import PartitionSpec as P

FFW = 1024
BLOCK = 128
CAP = 48
ROWS = 256
FEAT = 896
HALF = 8 * CAP
SLOTS = 2 * HALF
OUTS = 3
PARTS = 4
PCOLS = 2 * FFW // PARTS
MESH = pl.DeviceIdType.MESH
BF = jnp.bfloat16
F32 = jnp.float32


def kernel(
    grad, ids, stash, scale, weight,
    in_grad, weight_grad, parts,
    raw, out, rows, wts, hidden, coef, dh, dh_out, dh_in, back, ret, pick, pick_t, keys, fin_out, fin_in,
    raw_s, raw_r, key_s, key_r, w_s, w_r, x_s, x_r, hid_s, hid_r, dh_s, dh_r, part_s, part_r, ret_s, ret_r, fin_s, fin_r,
    own_sem, stash_sem, self_sem, load_sem,
):
    e = lax.axis_index("expert")
    f = lax.axis_index("fsdp")
    zh, x, c = e // 8, (e // 2) % 4, e % 2
    zl, y = f // 4, f % 4

    def z_peer(d):
        h = 1 - zh if d & 2 else zh
        l = 1 - zl if d & 1 else zl
        return (h * 8 + x * 2 + c, l * 4 + y)

    def xc(k, sign):
        dx, dc = k // 2, k % 2
        return lax.rem(x + (4 + sign * dx), 4), (1 - c if dc else c)

    def x_peer(k, sign):
        px, pc = xc(k, sign)
        return (zh * 8 + px * 2 + pc, f)

    def y_peer(j):
        return (e, zl * 4 + lax.rem(y + 4 + j, 4))

    def remote(src, dst, s, r, device):
        return pltpu.make_async_remote_copy(
            src_ref=src, dst_ref=dst, send_sem=s, recv_sem=r, device_id=device, device_id_type=MESH
        )

    barrier = pltpu.get_barrier_semaphore()
    peers = [z_peer(d) for d in (1, 2, 3)] + [x_peer(k, 1) for k in range(1, 8)] + [y_peer(j) for j in (1, 2, 3)]
    for peer in peers:
        pl.semaphore_signal(barrier, inc=1, device_id=peer, device_id_type=MESH)

    def columns(half, step):
        quarter = lax.rem(y + step, 4)
        return pl.ds(pl.multiple_of((half * 4 + quarter) * FEAT, 128), FEAT)

    stash_copies = []
    for s in range(16):
        sx, sc = xc(s % 8, -1)
        g = (1 - zh if s // 8 else zh) * 8 + sx * 2 + sc
        stash_copies.append(
            pltpu.make_async_copy(stash.at[0, 0, g], back.at[s // 8, pl.ds((s % 8) * CAP, CAP)], stash_sem.at[s])
        )
    own_weight = pltpu.make_async_copy(weight.at[0], wts.at[0], own_sem.at[4])
    own_rows = [
        pltpu.make_async_copy(grad.at[:, columns(zl, i + 1)], raw.at[0, i], own_sem.at[i]) for i in range(4)
    ]
    own_weight.start()
    for copy in stash_copies + own_rows:
        copy.start()

    expert_of = ids[...]
    same = lax.broadcasted_iota(jnp.int32, (16, ROWS), 0) == expert_of
    chosen = jnp.where(same, 1.0, 0.0)
    earlier = jnp.where(
        lax.broadcasted_iota(jnp.int32, (ROWS, ROWS), 0) < lax.broadcasted_iota(jnp.int32, (ROWS, ROWS), 1), 1.0, 0.0
    )
    count = jnp.dot(chosen.astype(BF), earlier.astype(BF), preferred_element_type=F32)
    slot = jnp.sum(chosen * count, axis=0, keepdims=True)
    key = expert_of * CAP + slot.astype(jnp.int32)
    keys[0] = jnp.broadcast_to(key, (8, ROWS))

    pl.semaphore_wait(barrier, len(peers))

    raw_copies = {}
    for i in range(4):
        for d in (1, 3):
            raw_copies[d, i] = remote(
                grad.at[:, columns(1 - zl, i)], raw.at[d, i], raw_s.at[d, i], raw_r.at[d, i], z_peer(d)
            )
        raw_copies[2, i] = remote(
            grad.at[:, columns(zl, i + 1)], raw.at[2, i], raw_s.at[2, i], raw_r.at[2, i], z_peer(2)
        )
    key_copies = [remote(keys.at[0], keys.at[d], key_s.at[d], key_r.at[d], z_peer(d)) for d in (1, 2, 3)]
    weight_copies = [remote(weight.at[0], wts.at[j], w_s.at[j], w_r.at[j], y_peer(-j)) for j in (1, 2, 3)]
    for copy in key_copies:
        copy.start()
    for i in range(4):
        raw_copies[1, i].start()
        raw_copies[3, i].start()
    for copy in weight_copies:
        copy.start()

    place = lax.broadcasted_iota(jnp.int32, (CAP, ROWS), 0)

    def make_pick(d):
        key_of = keys[d, 0:1, :]
        for k in range(8):
            px, pc = xc(k, 1)
            base = (zh * 8 + px * 2 + pc) * CAP
            pick[d, k * CAP : (k + 1) * CAP, :] = jnp.where(key_of - base == place, 1.0, 0.0).astype(BF)

    for copy in key_copies:
        copy.wait_recv()
    for d in range(4):
        make_pick(d)

    x_copies = {}

    def dispatch(s):
        group, i = s // 4, s % 4
        slot_of = s % OUTS
        if s >= OUTS:
            for copy in x_copies[s - OUTS]:
                copy.wait_send()
        for zr in range(2):
            d = 2 * zr + (1 - group)
            if d == 0:
                own_rows[i].wait()
            else:
                raw_copies[d, i].wait_recv()

            def tile(t, _, zr=zr, d=d):
                at = pl.ds(pl.multiple_of(t * 192, 192), 192)
                put = jnp.dot(pick[d, at, :], raw[d, i], preferred_element_type=F32)
                out[slot_of, zr, at, :] = put.astype(BF)
                return 0

            lax.fori_loop(0, 2, tile, 0)
            rows[group, i, zr, 0:CAP, :] = out[slot_of, zr, 0:CAP, :]
        x_copies[s] = []
        for k in range(1, 8):
            block = pl.ds(k * CAP, CAP)
            copy = remote(
                out.at[slot_of, :, block, :], rows.at[group, i, :, block, :], x_s.at[s, k], x_r.at[s, k], x_peer(k, 1)
            )
            copy.start()
            x_copies[s].append(copy)

    dispatch(0)
    dispatch(1)
    raw_copies[2, 0].start()
    raw_copies[2, 1].start()

    for copy in stash_copies:
        copy.wait()

    def gate_tile(s, _):
        zr, k = s // 8, s % 8
        dx, dc = k // 2, k % 2
        sx = lax.rem(x + 4 - dx, 4)
        sc = c + dc - 2 * c * dc
        sz = zh + zr - 2 * zh * zr
        factor = jnp.exp2(scale[sz * 8 + sx * 2 + sc].astype(F32))
        at = pl.ds(pl.multiple_of(k * CAP, CAP), CAP)
        flat = pl.ds(pl.multiple_of(s * CAP, CAP), CAP)
        for b in range(FFW // BLOCK):
            low, high = slice(b * BLOCK, (b + 1) * BLOCK), slice(FFW + b * BLOCK, FFW + (b + 1) * BLOCK)
            gate = back[zr, at, low].astype(F32) * factor[:, b : b + 1]
            up = back[zr, at, high].astype(F32) * factor[:, 8 + b : 9 + b]
            sig = 1.0 / (1.0 + jnp.exp(-gate))
            silu = gate * sig
            dh_out[flat, low] = (silu * up).astype(BF)
            coef[flat, low] = (up * sig * (1.0 + gate * (1.0 - sig))).astype(BF)
            coef[flat, high] = silu.astype(BF)
        return 0

    lax.fori_loop(0, 16, gate_tile, 0)

    def turn(b, _):
        at = pl.ds(pl.multiple_of(b * BLOCK, BLOCK), BLOCK)
        hidden[0, at, :] = dh_out[:, at].T
        return 0

    lax.fori_loop(0, FFW // BLOCK, turn, 0)
    for n, d in enumerate((0, 2)):
        pick_t[n] = pick[d].astype(F32).T.astype(BF)
    hidden_copy = remote(hidden.at[0], hidden.at[1], hid_s.at[0], hid_r.at[0], z_peer(1))
    hidden_copy.start()

    def d_hidden(group, i, w):
        def tile(n, _):
            at = pl.ds(pl.multiple_of(n * 256, 256), 256)
            term = lax.dot_general(
                rows[group, i].reshape(SLOTS, FEAT), wts[w, at, :], (((1,), (1,)), ((), ())), preferred_element_type=F32
            )
            if i == 0:
                dh[:, at] = term
            else:
                dh[:, at] += term
            return 0

        lax.fori_loop(0, FFW // 256, tile, 0)

    def partial(i, earlier_step, into):
        def tile(m, _):
            at = pl.ds(pl.multiple_of(m * 256, 256), 256)
            term = jnp.dot(hidden[0, at, :], rows[1, i].reshape(SLOTS, FEAT), preferred_element_type=F32)
            term += jnp.dot(hidden[1, at, :], rows[0, earlier_step].reshape(SLOTS, FEAT), preferred_element_type=F32)
            wts[into, at, :] = term.astype(BF)
            return 0

        lax.fori_loop(0, FFW // 256, tile, 0)

    part_copies = []
    dh_copy = remote(dh_out, dh_in, dh_s.at[0], dh_r.at[0], z_peer(1))
    for s in range(8):
        group, i = s // 4, s % 4
        for copy in x_copies[s]:
            copy.wait_recv()
        if group == 0:
            if i == 0:
                own_weight.wait()
            else:
                weight_copies[i - 1].wait_recv()
            d_hidden(0, i, i)
            if i == 3:
                dh_out[...] = dh[...].astype(BF)
                dh_copy.start()
        else:
            w = (1 + i) % 4
            d_hidden(1, i, w)
            if i == 0:
                hidden_copy.wait_recv()
            if i < 3:
                partial(i, w, w)
                copy = remote(wts.at[w], parts.at[i], part_s.at[i], part_r.at[i], y_peer(1 + i))
                copy.start()
                part_copies.append(copy)
        if s + 2 < 8:
            dispatch(s + 2)
        if s in (0, 1):
            raw_copies[2, 2 + s].start()

    dh_copy.wait_recv()
    ret_copies, self_copies, fin_copies = {}, [], []
    for p in range(PARTS):
        cols = pl.ds(p * PCOLS, PCOLS)
        dh_cols = pl.ds((p % 2) * PCOLS, PCOLS)

        def back_tile(s, _, cols=cols, dh_cols=dh_cols):
            at = pl.ds(pl.multiple_of((s % 8) * CAP, CAP), CAP)
            flat = pl.ds(pl.multiple_of(s * CAP, CAP), CAP)
            total = dh[flat, dh_cols] + dh_in[flat, dh_cols].astype(F32)
            back[s // 8, at, cols] = (total * coef[flat, cols].astype(F32)).astype(BF)
            return 0

        lax.fori_loop(0, 16, back_tile, 0)
        here = pltpu.make_async_copy(back.at[:, pl.ds(0, CAP), cols], ret.at[:, pl.ds(0, CAP), cols], self_sem.at[p])
        here.start()
        self_copies.append(here)
        ret_copies[p] = []
        for k in range(1, 8):
            block = pl.ds(k * CAP, CAP)
            copy = remote(
                back.at[:, block, cols], ret.at[:, block, cols], ret_s.at[p, k], ret_r.at[p, k], x_peer(k, -1)
            )
            copy.start()
            ret_copies[p].append(copy)

    partial(3, 0, 0)

    for p in range(PARTS):
        cols = pl.ds(p * PCOLS, PCOLS)
        self_copies[p].wait()
        for copy in ret_copies[p]:
            copy.wait_recv()
        fin_out[:, cols] = jnp.dot(pick_t[1], ret[1, :, cols], preferred_element_type=F32).astype(BF)
        copy = remote(fin_out.at[:, cols], fin_in.at[:, cols], fin_s.at[p], fin_r.at[p], z_peer(2))
        copy.start()
        fin_copies.append(copy)
        in_grad[:, cols] = jnp.dot(pick_t[0], ret[0, :, cols], preferred_element_type=F32).astype(BF)

    loads = []
    for i in range(3):
        part_copies[i].wait_recv()
        part_copies[i].wait_send()
        load = pltpu.make_async_copy(parts.at[i], wts.at[1 + i], load_sem.at[i])
        load.start()
        loads.append(load)
    for load in loads:
        load.wait()

    def sum_tile(t, _):
        at = pl.ds(pl.multiple_of(t * 64, 64), 64)
        total = wts[0, at, :].astype(F32)
        for i in range(1, 4):
            total += wts[i, at, :].astype(F32)
        weight_grad[0, at, :] = total.astype(BF)
        return 0

    lax.fori_loop(0, FFW // 64, sum_tile, 0)

    for p in range(PARTS):
        cols = pl.ds(p * PCOLS, PCOLS)
        fin_copies[p].wait_recv()
        in_grad[:, cols] = in_grad[:, cols] + fin_in[:, cols]

    sent = list(raw_copies.values()) + key_copies + weight_copies + [hidden_copy, dh_copy] + fin_copies
    for s in range(8 - OUTS, 8):
        sent += x_copies[s]
    for p in range(PARTS):
        sent += ret_copies[p]
    for copy in sent:
        copy.wait_send()


def shards(out_grad, expert_ids, stash_codes, stash_scale, down_weight):
    dma = pltpu.SemaphoreType.DMA
    hbm = pl.BlockSpec(memory_space=pl.ANY)
    vmem = pl.BlockSpec(memory_space=pltpu.VMEM)
    scratch = [
        pltpu.VMEM((4, 4, ROWS, FEAT), BF),
        pltpu.VMEM((OUTS, 2, HALF, FEAT), BF),
        pltpu.VMEM((2, 4, 2, HALF, FEAT), BF),
        pltpu.VMEM((4, FFW, FEAT), BF),
        pltpu.VMEM((2, FFW, SLOTS), BF),
        pltpu.VMEM((SLOTS, 2 * FFW), BF),
        pltpu.VMEM((SLOTS, FFW), F32),
        pltpu.VMEM((SLOTS, FFW), BF),
        pltpu.VMEM((SLOTS, FFW), BF),
        pltpu.VMEM((2, HALF, 2 * FFW), BF),
        pltpu.VMEM((2, HALF, 2 * FFW), BF),
        pltpu.VMEM((4, HALF, ROWS), BF),
        pltpu.VMEM((2, ROWS, HALF), BF),
        pltpu.VMEM((4, 8, ROWS), jnp.int32),
        pltpu.VMEM((ROWS, 2 * FFW), BF),
        pltpu.VMEM((ROWS, 2 * FFW), BF),
    ]
    pairs = [(4, 4), (4,), (4,), (8, 8), (1,), (1,), (3,), (PARTS, 8), (PARTS,)]
    for shape in pairs:
        scratch += [dma(shape), dma(shape)]
    scratch += [dma((5,)), dma((16,)), dma((PARTS,)), dma((3,))]
    in_grad, weight_grad, _ = pl.pallas_call(
        kernel,
        out_shape=(
            jax.ShapeDtypeStruct((ROWS, 2 * FFW), BF),
            jax.ShapeDtypeStruct((1, FFW, FEAT), BF),
            jax.ShapeDtypeStruct((3, FFW, FEAT), BF),
        ),
        in_specs=[hbm, vmem, hbm, vmem, hbm],
        out_specs=(vmem, vmem, hbm),
        scratch_shapes=scratch,
        compiler_params=pltpu.CompilerParams(
            collective_id=0, has_side_effects=True, vmem_limit_bytes=60 * 2**20
        ),
        name="expert_backward",
    )(out_grad, expert_ids.reshape(1, ROWS), stash_codes, stash_scale[0, 0], down_weight)
    return in_grad, weight_grad


def solution(mesh):
    placed = (
        P(("expert", "fsdp"), None),
        P(("expert", "fsdp"), None),
        P("expert", "fsdp", None, None, None),
        P("expert", "fsdp", None, None, None),
        P("expert", None, "fsdp"),
    )
    return jax.shard_map(
        shards,
        mesh=mesh,
        in_specs=placed,
        out_specs=(P(("expert", "fsdp"), None), P("expert", None, "fsdp")),
        check_vma=False,
    )
```

```python
import jax
import jax.numpy as jnp
from jax import lax
from jax.experimental import pallas as pl
from jax.experimental.pallas import tpu as pltpu
from jax.sharding import PartitionSpec as P

FFW = 1024
BLOCK = 128
CAP = 48
ROWS = 256
FEAT = 896
HALF = 8 * CAP
SLOTS = 2 * HALF
OUTS = 8
ORDER = (2, 1, 3, 0)
PARTS = 4
PCOLS = 2 * FFW // PARTS
MESH = pl.DeviceIdType.MESH
BF = jnp.bfloat16
F32 = jnp.float32


def kernel(
    grad, ids, stash, scale_in, weight,
    own_grad, far_grad, parts,
    raw, out, rows, wts, hidden, coef, dh, dh_out, dh_in, back, ret, pick, pick_t, keys, fin, scale,
    raw_s, raw_r, key_s, key_r, w_s, w_r, x_s, x_r, hid_s, hid_r, dh_s, dh_r, part_s, part_r, ret_s, ret_r, fin_s, fin_r,
    own_sem, stash_sem, self_sem, store_sem,
):
    e = lax.axis_index("expert")
    f = lax.axis_index("fsdp")
    zh, x, c = e // 8, (e // 2) % 4, e % 2
    zl, y = f // 4, f % 4

    def z_peer(d):
        h = 1 - zh if d & 2 else zh
        l = 1 - zl if d & 1 else zl
        return (h * 8 + x * 2 + c, l * 4 + y)

    def xc(k, sign):
        dx, dc = k // 2, k % 2
        return lax.rem(x + (4 + sign * dx), 4), (1 - c if dc else c)

    def x_peer(k, sign):
        px, pc = xc(k, sign)
        return (zh * 8 + px * 2 + pc, f)

    def y_peer(j):
        return (e, zl * 4 + lax.rem(y + 4 + j, 4))

    def remote(src, dst, s, r, device):
        return pltpu.make_async_remote_copy(
            src_ref=src, dst_ref=dst, send_sem=s, recv_sem=r, device_id=device, device_id_type=MESH
        )

    barrier = pltpu.get_barrier_semaphore()
    peers = [z_peer(d) for d in (1, 2, 3)] + [x_peer(k, 1) for k in range(1, 8)] + [y_peer(j) for j in (1, 2, 3)]
    for peer in peers:
        pl.semaphore_signal(barrier, inc=1, device_id=peer, device_id_type=MESH)

    def columns(half, j):
        quarter = lax.rem(y + j, 4)
        return pl.ds(pl.multiple_of((half * 4 + quarter) * FEAT, 128), FEAT)

    own_rows = {
        j: pltpu.make_async_copy(grad.at[:, columns(zl, j)], raw.at[0, j], own_sem.at[j]) for j in ORDER
    }
    stash_copies = [pltpu.make_async_copy(scale_in.at[0, 0], scale, own_sem.at[5])]
    for s in range(16):
        sx, sc = xc(s % 8, -1)
        g = (1 - zh if s // 8 else zh) * 8 + sx * 2 + sc
        stash_copies.append(
            pltpu.make_async_copy(stash.at[0, 0, g], back.at[s // 8, pl.ds((s % 8) * CAP, CAP)], stash_sem.at[s])
        )
    own_weight = pltpu.make_async_copy(weight.at[0], wts.at[0], own_sem.at[4])
    for j in ORDER:
        own_rows[j].start()
    for copy in stash_copies:
        copy.start()
    own_weight.start()

    expert_of = ids[...]
    same = lax.broadcasted_iota(jnp.int32, (16, ROWS), 0) == expert_of
    chosen = jnp.where(same, 1.0, 0.0)
    earlier = jnp.where(
        lax.broadcasted_iota(jnp.int32, (ROWS, ROWS), 0) < lax.broadcasted_iota(jnp.int32, (ROWS, ROWS), 1), 1.0, 0.0
    )
    count = jnp.dot(chosen.astype(BF), earlier.astype(BF), preferred_element_type=F32)
    slot = jnp.sum(chosen * count, axis=0, keepdims=True)
    key = expert_of * CAP + slot.astype(jnp.int32)
    keys[0] = jnp.broadcast_to(key, (8, ROWS))

    place = lax.broadcasted_iota(jnp.int32, (CAP, ROWS), 0)

    def make_pick(d):
        key_of = keys[d, 0:1, :]
        for k in range(8):
            px, pc = xc(k, 1)
            base = (zh * 8 + px * 2 + pc) * CAP
            pick[d, k * CAP : (k + 1) * CAP, :] = jnp.where(key_of - base == place, 1.0, 0.0).astype(BF)

    make_pick(0)
    pl.semaphore_wait(barrier, len(peers))

    raw_copies = {
        (d, j): remote(
            grad.at[:, columns(1 - zl if d & 1 else zl, j)], raw.at[d, j], raw_s.at[d, j], raw_r.at[d, j], z_peer(d)
        )
        for d in (1, 2, 3)
        for j in ORDER
    }
    key_copies = [remote(keys.at[0], keys.at[d], key_s.at[d], key_r.at[d], z_peer(d)) for d in (1, 2, 3)]
    weight_copies = {j: remote(weight.at[0], wts.at[j], w_s.at[j], w_r.at[j], y_peer(-j)) for j in (1, 2, 3)}
    hidden_copy = remote(hidden.at[0], hidden.at[1], hid_s.at[0], hid_r.at[0], z_peer(1))
    dh_copies = [remote(dh_out.at[zr], dh_in.at[zr], dh_s.at[zr], dh_r.at[zr], z_peer(1)) for zr in range(2)]
    part_copies = {
        j: remote(wts.at[j], parts.at[j - 1], part_s.at[j - 1], part_r.at[j - 1], y_peer(j)) for j in (1, 2, 3)
    }

    x_copies = {}
    order = []

    def dispatch(d, j):
        unit = len(order)
        into = unit % OUTS
        if unit >= OUTS:
            for copy in x_copies[order[unit - OUTS]]:
                copy.wait_send()
        order.append((d, j))
        if d == 0:
            own_rows[j].wait()
        else:
            raw_copies[d, j].wait_recv()

        def tile(t, _):
            at = pl.ds(pl.multiple_of(t * 192, 192), 192)
            out[into, at, :] = jnp.dot(pick[d, at, :], raw[d, j], preferred_element_type=F32).astype(BF)
            return 0

        lax.fori_loop(0, 2, tile, 0)
        rows[d, j, 0:CAP, :] = out[into, 0:CAP, :]
        x_copies[d, j] = []
        for k in range(1, 8):
            block = pl.ds(k * CAP, CAP)
            copy = remote(
                out.at[into, block, :], rows.at[d, j, block, :], x_s.at[unit, k], x_r.at[unit, k], x_peer(k, 1)
            )
            copy.start()
            x_copies[d, j].append(copy)

    def gate_tile(s, _):
        zr, k = s // 8, s % 8
        dx, dc = k // 2, k % 2
        sx = lax.rem(x + 4 - dx, 4)
        sc = c + dc - 2 * c * dc
        sz = zh + zr - 2 * zh * zr
        factor = jnp.exp2(scale[sz * 8 + sx * 2 + sc].astype(F32)).T
        at = pl.ds(pl.multiple_of(k * CAP, CAP), CAP)
        for b in range(FFW // BLOCK):
            low, high = slice(b * BLOCK, (b + 1) * BLOCK), slice(FFW + b * BLOCK, FFW + (b + 1) * BLOCK)
            gate = back[zr, at, low].astype(F32) * factor[:, b : b + 1]
            up = back[zr, at, high].astype(F32) * factor[:, 8 + b : 9 + b]
            sig = 1.0 / (1.0 + jnp.exp(-gate))
            silu = gate * sig
            dh_out[zr, at, low] = (silu * up).astype(BF)
            coef[zr, at, low] = (up * sig * (1.0 + gate * (1.0 - sig))).astype(BF)
            coef[zr, at, high] = silu.astype(BF)
        return 0

    def turn(b, _):
        at = pl.ds(pl.multiple_of(b * BLOCK, BLOCK), BLOCK)
        for zr in range(2):
            hidden[0, at, zr * HALF : (zr + 1) * HALF] = dh_out[zr, :, at].T
        return 0

    def d_hidden(d, j):
        for copy in x_copies[d, j]:
            copy.wait_recv()

        def tile(n, _):
            at = pl.ds(pl.multiple_of(n * 256, 256), 256)
            term = lax.dot_general(
                rows[d, j], wts[j, at, :], (((1,), (1,)), ((), ())), preferred_element_type=F32
            )
            if j == ORDER[0]:
                dh[d, :, at] = term
            else:
                dh[d, :, at] += term
            return 0

        lax.fori_loop(0, FFW // 256, tile, 0)

    def partial(j):
        def tile(m, _):
            at = pl.ds(pl.multiple_of(m * 256, 256), 256)
            term = jnp.dot(hidden[0, at, 0:HALF], rows[0, j], preferred_element_type=F32)
            term += jnp.dot(hidden[0, at, HALF:SLOTS], rows[2, j], preferred_element_type=F32)
            term += jnp.dot(hidden[1, at, 0:HALF], rows[1, j], preferred_element_type=F32)
            term += jnp.dot(hidden[1, at, HALF:SLOTS], rows[3, j], preferred_element_type=F32)
            wts[j, at, :] = term.astype(BF)
            return 0

        lax.fori_loop(0, FFW // 256, tile, 0)
        if j:
            part_copies[j].start()

    def exchange(zr):
        dh_out[zr] = dh[1 + 2 * zr].astype(BF)
        dh_copies[zr].start()

    ret_copies, self_copies, fin_copies, store_copies = {}, {}, [], []

    def send_back(zr):
        dh_copies[zr].wait_recv()
        for p in range(PARTS):
            cols = pl.ds(p * PCOLS, PCOLS)
            dh_cols = pl.ds((p * PCOLS) % FFW, PCOLS)

            def back_tile(k, _, cols=cols, dh_cols=dh_cols):
                at = pl.ds(pl.multiple_of(k * CAP, CAP), CAP)
                total = dh[2 * zr, at, dh_cols] + dh_in[zr, at, dh_cols].astype(F32)
                back[zr, at, cols] = (total * coef[zr, at, cols].astype(F32)).astype(BF)
                return 0

            lax.fori_loop(0, 8, back_tile, 0)
            here = pltpu.make_async_copy(
                back.at[zr, pl.ds(0, CAP), cols], ret.at[zr, pl.ds(0, CAP), cols], self_sem.at[zr, p]
            )
            here.start()
            self_copies[zr, p] = here
            ret_copies[zr, p] = []
            for k in range(1, 8):
                block = pl.ds(k * CAP, CAP)
                copy = remote(
                    back.at[zr, block, cols], ret.at[zr, block, cols],
                    ret_s.at[zr, p, k], ret_r.at[zr, p, k], x_peer(k, -1),
                )
                copy.start()
                ret_copies[zr, p].append(copy)

    def collect(zr, p):
        cols = pl.ds(p * PCOLS, PCOLS)
        self_copies[zr, p].wait()
        for copy in ret_copies[zr, p]:
            copy.wait_recv()
        fin[zr, :, cols] = jnp.dot(pick_t[zr], ret[zr, :, cols], preferred_element_type=F32).astype(BF)
        if zr:
            copy = remote(fin.at[1, :, cols], far_grad.at[:, cols], fin_s.at[p], fin_r.at[p], z_peer(2))
            fin_copies.append(copy)
        else:
            copy = pltpu.make_async_copy(fin.at[0, :, cols], own_grad.at[:, cols], store_sem.at[p])
            store_copies.append(copy)
        copy.start()

    a, b, g, o = ORDER
    for copy in key_copies:
        copy.start()
    for d in (1, 3, 2):
        raw_copies[d, a].start()
    weight_copies[a].start()
    dispatch(0, a)
    dispatch(0, b)
    for copy in key_copies:
        copy.wait_recv()
    for d in (1, 3, 2):
        make_pick(d)
    for copy in stash_copies:
        copy.wait()
    raw_copies[1, b].start()
    raw_copies[3, b].start()
    lax.fori_loop(0, 16, gate_tile, 0)
    dispatch(1, a)
    dispatch(3, a)
    lax.fori_loop(0, FFW // BLOCK, turn, 0)
    for n, d in enumerate((0, 2)):
        pick_t[n] = pick[d].astype(F32).T.astype(BF)
    dispatch(0, g)
    dispatch(2, a)
    raw_copies[2, b].start()
    hidden_copy.start()
    weight_copies[b].start()
    weight_copies[g].start()
    dispatch(1, b)
    raw_copies[1, g].start()
    dispatch(3, b)
    raw_copies[3, g].start()
    dispatch(0, o)
    dispatch(2, b)
    raw_copies[2, g].start()
    raw_copies[3, o].start()
    weight_copies[a].wait_recv()
    for d in (0, 1, 3, 2):
        d_hidden(d, a)
    dispatch(3, g)
    dispatch(3, o)
    raw_copies[1, o].start()
    hidden_copy.wait_recv()
    partial(a)
    weight_copies[b].wait_recv()
    for d in (0, 1, 3, 2):
        d_hidden(d, b)
    partial(b)
    dispatch(1, g)
    raw_copies[2, o].start()
    dispatch(2, g)
    weight_copies[g].wait_recv()
    own_weight.wait()
    d_hidden(0, g)
    d_hidden(0, o)
    d_hidden(3, g)
    d_hidden(3, o)
    exchange(1)
    dispatch(1, o)
    d_hidden(1, g)
    d_hidden(2, g)
    partial(g)
    dispatch(2, o)
    d_hidden(1, o)
    exchange(0)
    d_hidden(2, o)
    send_back(1)
    partial(o)
    store = pltpu.make_async_copy(wts.at[o], parts.at[3], own_sem.at[6])
    store.start()
    collect(1, 0)
    collect(1, 1)
    send_back(0)
    for p in range(2, PARTS):
        collect(1, p)
    for p in range(PARTS):
        collect(0, p)

    store.wait()
    for copy in store_copies:
        copy.wait()
    for copy in list(part_copies.values()) + fin_copies:
        copy.wait_recv()
    sent = list(raw_copies.values()) + key_copies + list(weight_copies.values()) + [hidden_copy] + dh_copies
    sent += list(part_copies.values()) + fin_copies
    for unit in order[len(order) - OUTS :]:
        sent += x_copies[unit]
    for copies in ret_copies.values():
        sent += copies
    for copy in sent:
        copy.wait_send()


def shards(out_grad, expert_ids, stash_codes, stash_scale, down_weight):
    dma = pltpu.SemaphoreType.DMA
    hbm = pl.BlockSpec(memory_space=pl.ANY)
    vmem = pl.BlockSpec(memory_space=pltpu.VMEM)
    scratch = [
        pltpu.VMEM((4, 4, ROWS, FEAT), BF),
        pltpu.VMEM((OUTS, HALF, FEAT), BF),
        pltpu.VMEM((4, 4, HALF, FEAT), BF),
        pltpu.VMEM((4, FFW, FEAT), BF),
        pltpu.VMEM((2, FFW, SLOTS), BF),
        pltpu.VMEM((2, HALF, 2 * FFW), BF),
        pltpu.VMEM((4, HALF, FFW), F32),
        pltpu.VMEM((2, HALF, FFW), BF),
        pltpu.VMEM((2, HALF, FFW), BF),
        pltpu.VMEM((2, HALF, 2 * FFW), BF),
        pltpu.VMEM((2, HALF, 2 * FFW), BF),
        pltpu.VMEM((4, HALF, ROWS), BF),
        pltpu.VMEM((2, ROWS, HALF), BF),
        pltpu.VMEM((4, 8, ROWS), jnp.int32),
        pltpu.VMEM((2, ROWS, 2 * FFW), BF),
        pltpu.VMEM((16, 16, CAP), jnp.int32),
    ]
    for shape in [(4, 4), (4,), (4,), (16, 8), (1,), (2,), (3,), (2, PARTS, 8), (PARTS,)]:
        scratch += [dma(shape), dma(shape)]
    scratch += [dma((7,)), dma((16,)), dma((2, PARTS)), dma((PARTS,))]
    own_grad, far_grad, parts = pl.pallas_call(
        kernel,
        out_shape=(
            jax.ShapeDtypeStruct((ROWS, 2 * FFW), BF),
            jax.ShapeDtypeStruct((ROWS, 2 * FFW), BF),
            jax.ShapeDtypeStruct((4, FFW, FEAT), BF),
        ),
        in_specs=[hbm, vmem, hbm, hbm, hbm],
        out_specs=(hbm, hbm, hbm),
        scratch_shapes=scratch,
        compiler_params=pltpu.CompilerParams(
            collective_id=0, has_side_effects=True, vmem_limit_bytes=60 * 2**20
        ),
        name="expert_backward",
    )(out_grad, expert_ids.reshape(1, ROWS), stash_codes, jnp.swapaxes(stash_scale, 3, 4), down_weight)
    weight_grad = jnp.sum(parts.astype(F32), axis=0).astype(BF)[None]
    return own_grad + far_grad, weight_grad


def solution(mesh):
    placed = (
        P(("expert", "fsdp"), None),
        P(("expert", "fsdp"), None),
        P("expert", "fsdp", None, None, None),
        P("expert", "fsdp", None, None, None),
        P("expert", None, "fsdp"),
    )
    return jax.shard_map(
        shards,
        mesh=mesh,
        in_specs=placed,
        out_specs=(P(("expert", "fsdp"), None), P("expert", None, "fsdp")),
        check_vma=False,
    )
```

```python
import jax
import jax.numpy as jnp
from jax import lax
from jax.experimental import pallas as pl
from jax.experimental.pallas import tpu as pltpu
from jax.sharding import PartitionSpec as P

FFW = 1024
BLOCK = 128
CAP = 48
ROWS = 256
FEAT = 896
HALF = 8 * CAP
SLOTS = 2 * HALF
OUTS = 6
ORDER = (2, 1, 3, 0)
PARTS = 4
PCOLS = 2 * FFW // PARTS
MESH = pl.DeviceIdType.MESH
BF = jnp.bfloat16
F32 = jnp.float32


def kernel(
    grad, ids, stash, scale_in, weight,
    own_grad, far_grad, weight_grad, parts,
    raw, merged, out, rows, wts, hidden, coef, dh, dh_out, dh_in, back, ret, pick, pick_t, keys, fin, scale,
    raw_s, raw_r, key_s, key_r, w_s, w_r, x_s, x_r, hid_s, hid_r, dh_s, dh_r, part_s, part_r, ret_s, ret_r, fin_s, fin_r,
    own_sem, other_sem, stash_sem, self_sem, store_sem, load_sem,
):
    e = lax.axis_index("expert")
    f = lax.axis_index("fsdp")
    zh, x, c = e // 8, (e // 2) % 4, e % 2
    zl, y = f // 4, f % 4

    def z_peer(d):
        h = 1 - zh if d & 2 else zh
        l = 1 - zl if d & 1 else zl
        return (h * 8 + x * 2 + c, l * 4 + y)

    def xc(k, sign):
        dx, dc = k // 2, k % 2
        return lax.rem(x + (4 + sign * dx), 4), (1 - c if dc else c)

    def x_peer(k, sign):
        px, pc = xc(k, sign)
        return (zh * 8 + px * 2 + pc, f)

    def y_peer(j):
        return (e, zl * 4 + lax.rem(y + 4 + j, 4))

    def remote(src, dst, s, r, device):
        return pltpu.make_async_remote_copy(
            src_ref=src, dst_ref=dst, send_sem=s, recv_sem=r, device_id=device, device_id_type=MESH
        )

    barrier = pltpu.get_barrier_semaphore()
    peers = [z_peer(d) for d in (1, 2, 3)] + [x_peer(k, 1) for k in range(1, 8)] + [y_peer(j) for j in (1, 2, 3)]
    for peer in peers:
        pl.semaphore_signal(barrier, inc=1, device_id=peer, device_id_type=MESH)

    def columns(half, j):
        quarter = lax.rem(y + j, 4)
        return pl.ds(pl.multiple_of((half * 4 + quarter) * FEAT, 128), FEAT)

    own_rows = {
        j: pltpu.make_async_copy(grad.at[:, columns(zl, j)], raw.at[0, j], own_sem.at[j]) for j in ORDER
    }
    stash_copies = [pltpu.make_async_copy(scale_in.at[0, 0], scale, own_sem.at[5])]
    for s in range(16):
        sx, sc = xc(s % 8, -1)
        g = (1 - zh if s // 8 else zh) * 8 + sx * 2 + sc
        stash_copies.append(
            pltpu.make_async_copy(stash.at[0, 0, g], back.at[s // 8, pl.ds((s % 8) * CAP, CAP)], stash_sem.at[s])
        )
    own_weight = pltpu.make_async_copy(weight.at[0], wts.at[0], own_sem.at[4])
    other_rows = {
        j: pltpu.make_async_copy(grad.at[:, columns(1 - zl, j)], merged.at[j], other_sem.at[j]) for j in ORDER
    }
    for j in ORDER:
        own_rows[j].start()
        other_rows[j].start()
    for copy in stash_copies:
        copy.start()
    own_weight.start()

    expert_of = ids[...]
    same = lax.broadcasted_iota(jnp.int32, (16, ROWS), 0) == expert_of
    chosen = jnp.where(same, 1.0, 0.0)
    earlier = jnp.where(
        lax.broadcasted_iota(jnp.int32, (ROWS, ROWS), 0) < lax.broadcasted_iota(jnp.int32, (ROWS, ROWS), 1), 1.0, 0.0
    )
    count = jnp.dot(chosen.astype(BF), earlier.astype(BF), preferred_element_type=F32)
    slot = jnp.sum(chosen * count, axis=0, keepdims=True)
    key = expert_of * CAP + slot.astype(jnp.int32)
    keys[0] = jnp.broadcast_to(key, (8, ROWS))

    place = lax.broadcasted_iota(jnp.int32, (CAP, ROWS), 0)

    def make_pick(d):
        key_of = keys[d, 0:1, :]
        for k in range(8):
            px, pc = xc(k, 1)
            base = (zh * 8 + px * 2 + pc) * CAP
            pick[d, k * CAP : (k + 1) * CAP, :] = jnp.where(key_of - base == place, 1.0, 0.0).astype(BF)

    make_pick(0)
    near = jnp.broadcast_to(expert_of // 8 == zh, (8, ROWS)).astype(F32).T[:, 0:1] > 0.5
    pl.semaphore_wait(barrier, len(peers))

    raw_copies = {}
    for j in ORDER:
        raw_copies[1, j] = remote(merged.at[j], raw.at[1, j], raw_s.at[1, j], raw_r.at[1, j], z_peer(1))
        raw_copies[2, j] = remote(raw.at[1, j], raw.at[2, j], raw_s.at[2, j], raw_r.at[2, j], z_peer(3))
        raw_copies[3, j] = remote(
            grad.at[:, columns(1 - zl, j)], raw.at[3, j], raw_s.at[3, j], raw_r.at[3, j], z_peer(3)
        )

    def merge(j):
        other_rows[j].wait()
        own_rows[j].wait()

        def tile(t, _):
            at = pl.ds(pl.multiple_of(t * BLOCK, BLOCK), BLOCK)
            merged[j, :, at] = jnp.where(near, merged[j, :, at].astype(F32), raw[0, j, :, at].astype(F32)).astype(BF)
            return 0

        lax.fori_loop(0, FEAT // BLOCK, tile, 0)
    key_copies = [remote(keys.at[0], keys.at[d], key_s.at[d], key_r.at[d], z_peer(d)) for d in (1, 2, 3)]
    weight_copies = {j: remote(weight.at[0], wts.at[j], w_s.at[j], w_r.at[j], y_peer(-j)) for j in (1, 3)}
    upper, lower = pl.ds(0, FFW // 2), pl.ds(FFW // 2, FFW // 2)
    weight_copies[0] = remote(wts.at[1, upper], wts.at[2, upper], w_s.at[0], w_r.at[0], y_peer(-1))
    weight_copies[2] = remote(wts.at[3, lower], wts.at[2, lower], w_s.at[2], w_r.at[2], y_peer(1))
    hidden_copy = remote(hidden.at[0], hidden.at[1], hid_s.at[0], hid_r.at[0], z_peer(1))
    dh_copies = [remote(dh_out.at[zr], dh_in.at[zr], dh_s.at[zr], dh_r.at[zr], z_peer(1)) for zr in range(2)]
    part_copies = {
        j: remote(wts.at[j], parts.at[j - 1], part_s.at[j - 1], part_r.at[j - 1], y_peer(j)) for j in (1, 2, 3)
    }

    x_copies = {}
    order = []

    def dispatch(d, j):
        unit = len(order)
        into = unit % OUTS
        if unit >= OUTS:
            for copy in x_copies[order[unit - OUTS]]:
                copy.wait_send()
        order.append((d, j))
        if d:
            raw_copies[d, j].wait_recv()
        if d == 1:
            raw_copies[2, j].start()

        def tile(t, _):
            at = pl.ds(pl.multiple_of(t * 192, 192), 192)
            out[into, at, :] = jnp.dot(pick[d, at, :], raw[d, j], preferred_element_type=F32).astype(BF)
            return 0

        lax.fori_loop(0, 2, tile, 0)
        rows[d, j, 0:CAP, :] = out[into, 0:CAP, :]
        x_copies[d, j] = []
        for k in range(1, 8):
            block = pl.ds(k * CAP, CAP)
            copy = remote(
                out.at[into, block, :], rows.at[d, j, block, :], x_s.at[unit, k], x_r.at[unit, k], x_peer(k, 1)
            )
            copy.start()
            x_copies[d, j].append(copy)

    def gate_tile(s, _):
        zr, k = s // 8, s % 8
        dx, dc = k // 2, k % 2
        sx = lax.rem(x + 4 - dx, 4)
        sc = c + dc - 2 * c * dc
        sz = zh + zr - 2 * zh * zr
        factor = jnp.exp2(scale[sz * 8 + sx * 2 + sc].astype(F32)).T
        at = pl.ds(pl.multiple_of(k * CAP, CAP), CAP)
        for b in range(FFW // BLOCK):
            low, high = slice(b * BLOCK, (b + 1) * BLOCK), slice(FFW + b * BLOCK, FFW + (b + 1) * BLOCK)
            gate = back[zr, at, low].astype(F32) * factor[:, b : b + 1]
            up = back[zr, at, high].astype(F32) * factor[:, 8 + b : 9 + b]
            sig = 1.0 / (1.0 + jnp.exp(-gate))
            silu = gate * sig
            dh_out[zr, at, low] = (silu * up).astype(BF)
            coef[zr, at, low] = (up * sig * (1.0 + gate * (1.0 - sig))).astype(BF)
            coef[zr, at, high] = silu.astype(BF)
        return 0

    def turn(b, _):
        at = pl.ds(pl.multiple_of(b * BLOCK, BLOCK), BLOCK)
        for zr in range(2):
            hidden[0, at, zr * HALF : (zr + 1) * HALF] = dh_out[zr, :, at].T
        return 0

    def d_hidden(d, j):
        for copy in x_copies[d, j]:
            copy.wait_recv()

        def tile(n, _):
            at = pl.ds(pl.multiple_of(n * 256, 256), 256)
            term = lax.dot_general(
                rows[d, j], wts[j, at, :], (((1,), (1,)), ((), ())), preferred_element_type=F32
            )
            if j == ORDER[0]:
                dh[d, :, at] = term
            else:
                dh[d, :, at] += term
            return 0

        lax.fori_loop(0, FFW // 256, tile, 0)

    def partial(j):
        def tile(m, _):
            at = pl.ds(pl.multiple_of(m * 256, 256), 256)
            term = jnp.dot(hidden[0, at, 0:HALF], rows[0, j], preferred_element_type=F32)
            term += jnp.dot(hidden[0, at, HALF:SLOTS], rows[2, j], preferred_element_type=F32)
            term += jnp.dot(hidden[1, at, 0:HALF], rows[1, j], preferred_element_type=F32)
            term += jnp.dot(hidden[1, at, HALF:SLOTS], rows[3, j], preferred_element_type=F32)
            wts[j, at, :] = term.astype(BF)
            return 0

        lax.fori_loop(0, FFW // 256, tile, 0)
        if j:
            part_copies[j].start()

    def exchange(zr):
        dh_out[zr] = dh[1 + 2 * zr].astype(BF)
        dh_copies[zr].start()

    ret_copies, self_copies, fin_copies, store_copies = {}, {}, [], []

    def send_back(zr):
        dh_copies[zr].wait_recv()
        for p in range(PARTS):
            cols = pl.ds(p * PCOLS, PCOLS)
            dh_cols = pl.ds((p * PCOLS) % FFW, PCOLS)

            def back_tile(k, _, cols=cols, dh_cols=dh_cols):
                at = pl.ds(pl.multiple_of(k * CAP, CAP), CAP)
                total = dh[2 * zr, at, dh_cols] + dh_in[zr, at, dh_cols].astype(F32)
                back[zr, at, cols] = (total * coef[zr, at, cols].astype(F32)).astype(BF)
                return 0

            lax.fori_loop(0, 8, back_tile, 0)
            here = pltpu.make_async_copy(
                back.at[zr, pl.ds(0, CAP), cols], ret.at[zr, pl.ds(0, CAP), cols], self_sem.at[zr, p]
            )
            here.start()
            self_copies[zr, p] = here
            ret_copies[zr, p] = []
            for k in range(1, 8):
                block = pl.ds(k * CAP, CAP)
                copy = remote(
                    back.at[zr, block, cols], ret.at[zr, block, cols],
                    ret_s.at[zr, p, k], ret_r.at[zr, p, k], x_peer(k, -1),
                )
                copy.start()
                ret_copies[zr, p].append(copy)

    def collect(zr, p):
        cols = pl.ds(p * PCOLS, PCOLS)
        self_copies[zr, p].wait()
        for copy in ret_copies[zr, p]:
            copy.wait_recv()
        fin[zr, :, cols] = jnp.dot(pick_t[zr], ret[zr, :, cols], preferred_element_type=F32).astype(BF)
        if zr:
            copy = remote(fin.at[1, :, cols], far_grad.at[:, cols], fin_s.at[p], fin_r.at[p], z_peer(2))
            fin_copies.append(copy)
        else:
            copy = pltpu.make_async_copy(fin.at[0, :, cols], own_grad.at[:, cols], store_sem.at[p])
            store_copies.append(copy)
        copy.start()

    def collect_part(j):
        part_copies[j].wait_recv()
        part_copies[j].wait_send()
        load = pltpu.make_async_copy(parts.at[j - 1], wts.at[j], load_sem.at[j])
        load.start()
        return load

    a, b, g, o = ORDER
    for copy in key_copies:
        copy.start()
    raw_copies[3, a].start()
    weight_copies[1].start()
    weight_copies[3].start()
    merge(a)
    raw_copies[1, a].start()
    dispatch(0, a)
    merge(b)
    raw_copies[1, b].start()
    raw_copies[3, b].start()
    dispatch(0, b)
    merge(g)
    merge(o)
    for copy in key_copies:
        copy.wait_recv()
    for d in (1, 3, 2):
        make_pick(d)
    for copy in stash_copies:
        copy.wait()
    lax.fori_loop(0, 16, gate_tile, 0)
    dispatch(1, a)
    dispatch(3, a)
    raw_copies[1, g].start()
    raw_copies[3, g].start()
    lax.fori_loop(0, FFW // BLOCK, turn, 0)
    hidden_copy.start()
    for n, d in enumerate((0, 2)):
        pick_t[n] = pick[d].astype(F32).T.astype(BF)
    dispatch(2, a)
    dispatch(1, b)
    raw_copies[1, o].start()
    dispatch(3, b)
    raw_copies[3, o].start()
    weight_copies[1].wait_recv()
    weight_copies[0].start()
    weight_copies[3].wait_recv()
    weight_copies[2].start()
    dispatch(2, b)
    dispatch(1, g)
    dispatch(3, g)
    dispatch(0, g)
    weight_copies[0].wait_recv()
    weight_copies[2].wait_recv()
    for d in (0, 1, 3, 2):
        d_hidden(d, a)
    dispatch(3, o)
    hidden_copy.wait_recv()
    partial(a)
    dispatch(1, o)
    for d in (0, 1, 3, 2):
        d_hidden(d, b)
    weight_copies[0].wait_send()
    partial(b)
    dispatch(2, g)
    own_weight.wait()
    d_hidden(1, g)
    d_hidden(3, g)
    d_hidden(3, o)
    exchange(1)
    dispatch(0, o)
    dispatch(2, o)
    d_hidden(1, o)
    exchange(0)
    d_hidden(0, g)
    d_hidden(2, g)
    weight_copies[2].wait_send()
    partial(g)
    d_hidden(0, o)
    d_hidden(2, o)
    send_back(1)
    partial(o)
    loads = [collect_part(a)]
    collect(1, 0)
    collect(1, 1)
    send_back(0)
    for p in range(2, PARTS):
        collect(1, p)
    for p in range(PARTS):
        collect(0, p)
    loads += [collect_part(b), collect_part(g)]
    for load in loads:
        load.wait()

    def sum_tile(t, _):
        at = pl.ds(pl.multiple_of(t * 64, 64), 64)
        total = wts[0, at, :].astype(F32)
        for j in range(1, 4):
            total += wts[j, at, :].astype(F32)
        wts[0, at, :] = total.astype(BF)
        return 0

    lax.fori_loop(0, FFW // 64, sum_tile, 0)
    store = pltpu.make_async_copy(wts.at[0], weight_grad.at[0], own_sem.at[6])
    store.start()

    store.wait()
    for copy in store_copies:
        copy.wait()
    for copy in fin_copies:
        copy.wait_recv()
    sent = list(raw_copies.values()) + key_copies + [weight_copies[1], weight_copies[3]] + [hidden_copy] + dh_copies
    sent += fin_copies
    for unit in order[len(order) - OUTS :]:
        sent += x_copies[unit]
    for copies in ret_copies.values():
        sent += copies
    for copy in sent:
        copy.wait_send()


def shards(out_grad, expert_ids, stash_codes, stash_scale, down_weight):
    dma = pltpu.SemaphoreType.DMA
    hbm = pl.BlockSpec(memory_space=pl.ANY)
    vmem = pl.BlockSpec(memory_space=pltpu.VMEM)
    scratch = [
        pltpu.VMEM((4, 4, ROWS, FEAT), BF),
        pltpu.VMEM((4, ROWS, FEAT), BF),
        pltpu.VMEM((OUTS, HALF, FEAT), BF),
        pltpu.VMEM((4, 4, HALF, FEAT), BF),
        pltpu.VMEM((4, FFW, FEAT), BF),
        pltpu.VMEM((2, FFW, SLOTS), BF),
        pltpu.VMEM((2, HALF, 2 * FFW), BF),
        pltpu.VMEM((4, HALF, FFW), F32),
        pltpu.VMEM((2, HALF, FFW), BF),
        pltpu.VMEM((2, HALF, FFW), BF),
        pltpu.VMEM((2, HALF, 2 * FFW), BF),
        pltpu.VMEM((2, HALF, 2 * FFW), BF),
        pltpu.VMEM((4, HALF, ROWS), BF),
        pltpu.VMEM((2, ROWS, HALF), BF),
        pltpu.VMEM((4, 8, ROWS), jnp.int32),
        pltpu.VMEM((2, ROWS, 2 * FFW), BF),
        pltpu.VMEM((16, 16, CAP), jnp.int32),
    ]
    for shape in [(4, 4), (4,), (4,), (16, 8), (1,), (2,), (3,), (2, PARTS, 8), (PARTS,)]:
        scratch += [dma(shape), dma(shape)]
    scratch += [dma((7,)), dma((4,)), dma((16,)), dma((2, PARTS)), dma((PARTS,)), dma((4,))]
    own_grad, far_grad, weight_grad, _ = pl.pallas_call(
        kernel,
        out_shape=(
            jax.ShapeDtypeStruct((ROWS, 2 * FFW), BF),
            jax.ShapeDtypeStruct((ROWS, 2 * FFW), BF),
            jax.ShapeDtypeStruct((1, FFW, FEAT), BF),
            jax.ShapeDtypeStruct((3, FFW, FEAT), BF),
        ),
        in_specs=[hbm, vmem, hbm, hbm, hbm],
        out_specs=(hbm, hbm, hbm, hbm),
        scratch_shapes=scratch,
        compiler_params=pltpu.CompilerParams(
            collective_id=0, has_side_effects=True, vmem_limit_bytes=60 * 2**20
        ),
        name="expert_backward",
    )(out_grad, expert_ids.reshape(1, ROWS), stash_codes, jnp.swapaxes(stash_scale, 3, 4), down_weight)
    return own_grad + far_grad, weight_grad


def solution(mesh):
    placed = (
        P(("expert", "fsdp"), None),
        P(("expert", "fsdp"), None),
        P("expert", "fsdp", None, None, None),
        P("expert", "fsdp", None, None, None),
        P("expert", None, "fsdp"),
    )
    return jax.shard_map(
        shards,
        mesh=mesh,
        in_specs=placed,
        out_specs=(P(("expert", "fsdp"), None), P("expert", None, "fsdp")),
        check_vma=False,
    )
```

```python
import jax
import jax.numpy as jnp
from jax import lax
from jax.experimental import pallas as pl
from jax.experimental.pallas import tpu as pltpu
from jax.sharding import PartitionSpec as P

FFW = 1024
BLOCK = 128
CAP = 48
ROWS = 256
FEAT = 896
HALF = 8 * CAP
SLOTS = 2 * HALF
OUTS = 6
PLACE = (0, 2, 1, 3)
ORDER = (2, 1, 3, 0)
PARTS = 4
PCOLS = 2 * FFW // PARTS
MESH = pl.DeviceIdType.MESH
BF = jnp.bfloat16
F32 = jnp.float32


def kernel(
    grad, ids, stash, scale_in, weight,
    own_grad, far_grad, weight_grad, parts,
    raw, merged, out, rows, wts, far_part, far_in, hidden, coef, dh, dh_out, dh_in, back, ret, pick, pick_t, keys, fin, scale,
    raw_s, raw_r, key_s, key_r, w_s, w_r, x_s, x_r, hid_s, hid_r, dh_s, dh_r, far_s, far_r, part_s, part_r, ret_s, ret_r, fin_s, fin_r,
    own_sem, other_sem, stash_sem, self_sem, store_sem, load_sem,
):
    e = lax.axis_index("expert")
    f = lax.axis_index("fsdp")
    zh, x, c = e // 8, (e // 2) % 4, e % 2
    zl, y = f // 4, f % 4

    def z_peer(d):
        h = 1 - zh if d & 2 else zh
        l = 1 - zl if d & 1 else zl
        return (h * 8 + x * 2 + c, l * 4 + y)

    def xc(k, sign):
        dx, dc = k // 2, k % 2
        return lax.rem(x + (4 + sign * dx), 4), (1 - c if dc else c)

    def x_peer(k, sign):
        px, pc = xc(k, sign)
        return (zh * 8 + px * 2 + pc, f)

    def y_peer(j):
        return (e, zl * 4 + lax.rem(y + 4 + j, 4))

    def remote(src, dst, s, r, device):
        return pltpu.make_async_remote_copy(
            src_ref=src, dst_ref=dst, send_sem=s, recv_sem=r, device_id=device, device_id_type=MESH
        )

    barrier = pltpu.get_barrier_semaphore()
    peers = [z_peer(d) for d in (1, 2, 3)] + [x_peer(k, 1) for k in range(1, 8)] + [y_peer(j) for j in (1, 2, 3)]
    for peer in peers:
        pl.semaphore_signal(barrier, inc=1, device_id=peer, device_id_type=MESH)

    def columns(half, j):
        quarter = lax.rem(y + j, 4)
        return pl.ds(pl.multiple_of((half * 4 + quarter) * FEAT, 128), FEAT)

    own_rows = {
        j: pltpu.make_async_copy(grad.at[:, columns(zl, j)], raw.at[0, j], own_sem.at[j]) for j in ORDER
    }
    other_rows = {
        j: pltpu.make_async_copy(grad.at[:, columns(1 - zl, j)], merged.at[j], other_sem.at[j]) for j in ORDER
    }
    stash_copies = [pltpu.make_async_copy(scale_in.at[0, 0], scale, own_sem.at[5])]
    for s in range(16):
        sx, sc = xc(s % 8, -1)
        g = (1 - zh if s // 8 else zh) * 8 + sx * 2 + sc
        stash_copies.append(
            pltpu.make_async_copy(stash.at[0, 0, g], back.at[s // 8, pl.ds((s % 8) * CAP, CAP)], stash_sem.at[s])
        )
    own_weight = pltpu.make_async_copy(weight.at[0], wts.at[0], own_sem.at[4])
    for j in ORDER:
        own_rows[j].start()
        other_rows[j].start()

    expert_of = ids[...]
    same = lax.broadcasted_iota(jnp.int32, (16, ROWS), 0) == expert_of
    chosen = jnp.where(same, 1.0, 0.0)
    earlier = jnp.where(
        lax.broadcasted_iota(jnp.int32, (ROWS, ROWS), 0) < lax.broadcasted_iota(jnp.int32, (ROWS, ROWS), 1), 1.0, 0.0
    )
    count = jnp.dot(chosen.astype(BF), earlier.astype(BF), preferred_element_type=F32)
    slot = jnp.sum(chosen * count, axis=0, keepdims=True)
    key = expert_of * CAP + slot.astype(jnp.int32)
    keys[0] = jnp.broadcast_to(key, (8, ROWS))

    place = lax.broadcasted_iota(jnp.int32, (CAP, ROWS), 0)

    def make_pick(d):
        key_of = keys[d, 0:1, :]
        for k in range(8):
            px, pc = xc(k, 1)
            base = (zh * 8 + px * 2 + pc) * CAP
            pick[d, k * CAP : (k + 1) * CAP, :] = jnp.where(key_of - base == place, 1.0, 0.0).astype(BF)

    make_pick(0)
    near = jnp.broadcast_to(expert_of // 8 == zh, (8, ROWS)).astype(F32).T[:, 0:1] > 0.5

    raw_copies = {}
    for j in ORDER:
        raw_copies[1, j] = remote(merged.at[j], raw.at[1, j], raw_s.at[1, j], raw_r.at[1, j], z_peer(1))
        raw_copies[2, j] = remote(raw.at[1, j], raw.at[2, j], raw_s.at[2, j], raw_r.at[2, j], z_peer(3))
        raw_copies[3, j] = remote(
            grad.at[:, columns(1 - zl, j)], raw.at[3, j], raw_s.at[3, j], raw_r.at[3, j], z_peer(3)
        )

    loaded = []

    def own_ready(j):
        if j not in loaded:
            loaded.append(j)
            own_rows[j].wait()

    def merge(j):
        other_rows[j].wait()
        own_ready(j)

        def tile(t, _):
            at = pl.ds(pl.multiple_of(t * BLOCK, BLOCK), BLOCK)
            merged[j, :, at] = jnp.where(near, merged[j, :, at].astype(F32), raw[0, j, :, at].astype(F32)).astype(BF)
            return 0

        lax.fori_loop(0, FEAT // BLOCK, tile, 0)
    key_copies = [remote(keys.at[0], keys.at[d], key_s.at[d], key_r.at[d], z_peer(d)) for d in (1, 2, 3)]
    weight_copies = {j: remote(weight.at[0], wts.at[j], w_s.at[j], w_r.at[j], y_peer(-j)) for j in (1, 3)}
    upper, lower = pl.ds(0, FFW // 2), pl.ds(FFW // 2, FFW // 2)
    weight_copies[0] = remote(wts.at[1, upper], wts.at[2, upper], w_s.at[0], w_r.at[0], y_peer(-1))
    weight_copies[2] = remote(wts.at[3, lower], wts.at[2, lower], w_s.at[2], w_r.at[2], y_peer(1))
    hidden_copy = remote(hidden.at[:, pl.ds(0, SLOTS)], hidden.at[:, pl.ds(SLOTS, SLOTS)], hid_s.at[0], hid_r.at[0], z_peer(1))
    dh_copies = [remote(dh_out.at[zr], dh_in.at[zr], dh_s.at[zr], dh_r.at[zr], z_peer(1)) for zr in range(2)]
    far_copies = [
        remote(far_part.at[half], far_in.at[n], far_s.at[n], far_r.at[n], y_peer(1 - 2 * n))
        for n, half in enumerate((upper, lower))
    ]
    part_copies = {
        j: remote(wts.at[j], parts.at[j // 2], part_s.at[j // 2], part_r.at[j // 2], y_peer(j)) for j in (1, 3)
    }

    x_copies = {}
    order = []

    def put(d, j):
        unit = len(order)
        into = unit % OUTS
        if unit >= OUTS:
            for copy in x_copies[order[unit - OUTS]]:
                copy.wait_send()
        order.append((d, j))
        if d:
            raw_copies[d, j].wait_recv()
        else:
            own_ready(j)
        if d == 1:
            raw_copies[2, j].start()

        def tile(t, _):
            at = pl.ds(pl.multiple_of(t * 192, 192), 192)
            out[into, at, :] = jnp.dot(pick[d, at, :], raw[d, j], preferred_element_type=F32).astype(BF)
            return 0

        lax.fori_loop(0, 2, tile, 0)
        rows[j, PLACE[d], 0:CAP, :] = out[into, 0:CAP, :]

    def dispatch(d, j):
        if (d, j) not in order:
            put(d, j)
        unit = order.index((d, j))
        into = unit % OUTS
        x_copies[d, j] = []
        for k in range(1, 8):
            block = pl.ds(k * CAP, CAP)
            copy = remote(
                out.at[into, block, :], rows.at[j, PLACE[d], block, :], x_s.at[unit, k], x_r.at[unit, k], x_peer(k, 1)
            )
            copy.start()
            x_copies[d, j].append(copy)

    def gate_tile(s, _):
        zr, k = s // 8, s % 8
        dx, dc = k // 2, k % 2
        sx = lax.rem(x + 4 - dx, 4)
        sc = c + dc - 2 * c * dc
        sz = zh + zr - 2 * zh * zr
        factor = jnp.exp2(scale[sz * 8 + sx * 2 + sc].astype(F32)).T
        at = pl.ds(pl.multiple_of(k * CAP, CAP), CAP)
        for b in range(FFW // BLOCK):
            low, high = slice(b * BLOCK, (b + 1) * BLOCK), slice(FFW + b * BLOCK, FFW + (b + 1) * BLOCK)
            gate = back[zr, at, low].astype(F32) * factor[:, b : b + 1]
            up = back[zr, at, high].astype(F32) * factor[:, 8 + b : 9 + b]
            sig = 1.0 / (1.0 + jnp.exp(-gate))
            silu = gate * sig
            dh_out[zr, at, low] = (silu * up).astype(BF)
            coef[zr, at, low] = (up * sig * (1.0 + gate * (1.0 - sig))).astype(BF)
            coef[zr, at, high] = silu.astype(BF)
        return 0

    def turn(b, _):
        at = pl.ds(pl.multiple_of(b * BLOCK, BLOCK), BLOCK)
        for zr in range(2):
            hidden[at, zr * HALF : (zr + 1) * HALF] = dh_out[zr, :, at].T
        return 0

    def arrived(j, sources):
        for d in sources:
            for copy in x_copies[d, j]:
                copy.wait_recv()

    def d_hidden(d, j):
        arrived(j, (d,))

        def tile(n, _):
            at = pl.ds(pl.multiple_of(n * 256, 256), 256)
            dh[PLACE[d], :, at] += lax.dot_general(
                rows[j, PLACE[d]], wts[j, at, :], (((1,), (1,)), ((), ())), preferred_element_type=F32
            )
            return 0

        lax.fori_loop(0, FFW // 256, tile, 0)

    def d_hidden_all(j, start):
        def tile(n, _):
            at = pl.ds(pl.multiple_of(n * 256, 256), 256)
            term = lax.dot_general(
                rows[j].reshape(2 * SLOTS, FEAT), wts[j, at, :], (((1,), (1,)), ((), ())), preferred_element_type=F32
            ).reshape(4, HALF, 256)
            dh[:, :, at] = term if start else dh[:, :, at] + term
            return 0

        lax.fori_loop(0, FFW // 256, tile, 0)

    def partial(j):
        into = far_part if j == 2 else wts.at[j]
        for n in range(2):

            def tile(m, _, n=n):
                at = pl.ds(pl.multiple_of(n * (FFW // 2) + m * 256, 256), 256)
                term = jnp.dot(hidden[at, :], rows[j].reshape(2 * SLOTS, FEAT), preferred_element_type=F32)
                if j == 1 + 2 * n:
                    term += far_in[n, pl.ds(pl.multiple_of(m * 256, 256), 256), :].astype(F32)
                into[at, :] = term.astype(BF)
                return 0

            if j == 1 + 2 * n:
                far_copies[n].wait_recv()
            lax.fori_loop(0, 2, tile, 0)
            if j == 2:
                far_copies[n].start()
        if j in (1, 3):
            part_copies[j].start()

    def exchange(zr):
        dh_out[zr] = dh[PLACE[1 + 2 * zr]].astype(BF)
        dh_copies[zr].start()

    ret_copies, self_copies, fin_copies, store_copies = {}, {}, [], []

    def send_back(zr):
        dh_copies[zr].wait_recv()
        for p in range(PARTS):
            cols = pl.ds(p * PCOLS, PCOLS)
            dh_cols = pl.ds((p * PCOLS) % FFW, PCOLS)

            def back_tile(k, _, cols=cols, dh_cols=dh_cols):
                at = pl.ds(pl.multiple_of(k * CAP, CAP), CAP)
                total = dh[PLACE[2 * zr], at, dh_cols] + dh_in[zr, at, dh_cols].astype(F32)
                back[zr, at, cols] = (total * coef[zr, at, cols].astype(F32)).astype(BF)
                return 0

            lax.fori_loop(0, 8, back_tile, 0)
            here = pltpu.make_async_copy(
                back.at[zr, pl.ds(0, CAP), cols], ret.at[zr, pl.ds(0, CAP), cols], self_sem.at[zr, p]
            )
            here.start()
            self_copies[zr, p] = here
            ret_copies[zr, p] = []
            for k in range(1, 8):
                block = pl.ds(k * CAP, CAP)
                copy = remote(
                    back.at[zr, block, cols], ret.at[zr, block, cols],
                    ret_s.at[zr, p, k], ret_r.at[zr, p, k], x_peer(k, -1),
                )
                copy.start()
                ret_copies[zr, p].append(copy)

    def collect(zr, p):
        cols = pl.ds(p * PCOLS, PCOLS)
        self_copies[zr, p].wait()
        for copy in ret_copies[zr, p]:
            copy.wait_recv()
        fin[zr, :, cols] = jnp.dot(pick_t[zr], ret[zr, :, cols], preferred_element_type=F32).astype(BF)
        if zr:
            copy = remote(fin.at[1, :, cols], far_grad.at[:, cols], fin_s.at[p], fin_r.at[p], z_peer(2))
            fin_copies.append(copy)
        else:
            copy = pltpu.make_async_copy(fin.at[0, :, cols], own_grad.at[:, cols], store_sem.at[p])
            store_copies.append(copy)
        copy.start()

    def collect_part(j):
        part_copies[j].wait_recv()
        part_copies[j].wait_send()
        load = pltpu.make_async_copy(parts.at[j // 2], wts.at[j], load_sem.at[j])
        load.start()
        return load

    a, b, g, o = ORDER
    put(0, a)
    merge(a)
    pl.semaphore_wait(barrier, len(peers))
    dispatch(0, a)
    raw_copies[1, a].start()
    raw_copies[3, a].start()
    for copy in key_copies:
        copy.start()
    weight_copies[1].start()
    weight_copies[3].start()
    merge(b)
    raw_copies[1, b].start()
    raw_copies[3, b].start()
    dispatch(0, b)
    merge(g)
    merge(o)
    for copy in stash_copies:
        copy.start()
    own_weight.start()
    for copy in key_copies:
        copy.wait_recv()
    for d in (1, 3, 2):
        make_pick(d)
    for copy in stash_copies:
        copy.wait()
    lax.fori_loop(0, 16, gate_tile, 0)
    dispatch(1, a)
    dispatch(3, a)
    raw_copies[3, g].start()
    lax.fori_loop(0, FFW // BLOCK, turn, 0)
    hidden_copy.start()
    for n, d in enumerate((0, 2)):
        pick_t[n] = pick[d].astype(F32).T.astype(BF)
    dispatch(2, a)
    dispatch(1, b)
    dispatch(3, b)
    raw_copies[3, o].start()
    dispatch(2, b)
    raw_copies[1, g].start()
    weight_copies[1].wait_recv()
    weight_copies[0].start()
    weight_copies[3].wait_recv()
    weight_copies[2].start()
    dispatch(0, g)
    dispatch(3, g)
    dispatch(3, o)
    raw_copies[1, o].start()
    arrived(a, (0, 1, 3, 2))
    hidden_copy.wait_recv()
    partial(a)
    dispatch(1, g)
    arrived(b, (0, 1, 3, 2))
    d_hidden_all(b, True)
    dispatch(2, g)
    weight_copies[0].wait_recv()
    weight_copies[2].wait_recv()
    d_hidden_all(a, False)
    own_weight.wait()
    d_hidden(3, g)
    d_hidden(3, o)
    exchange(1)
    dispatch(1, o)
    dispatch(2, o)
    dispatch(0, o)
    weight_copies[0].wait_send()
    partial(b)
    d_hidden(0, g)
    d_hidden(1, g)
    d_hidden(2, g)
    weight_copies[2].wait_send()
    partial(g)
    d_hidden(1, o)
    exchange(0)
    d_hidden(2, o)
    send_back(1)
    d_hidden(0, o)
    collect(1, 0)
    send_back(0)
    partial(o)
    for p in range(1, PARTS):
        collect(1, p)
    for p in range(PARTS - 1):
        collect(0, p)
    loads = [collect_part(b), collect_part(g)]
    for load in loads:
        load.wait()

    def sum_tile(t, _):
        at = pl.ds(pl.multiple_of(t * 64, 64), 64)
        total = wts[0, at, :].astype(F32)
        for j in (1, 3):
            total += wts[j, at, :].astype(F32)
        wts[0, at, :] = total.astype(BF)
        return 0

    lax.fori_loop(0, FFW // 64, sum_tile, 0)
    store = pltpu.make_async_copy(wts.at[0], weight_grad.at[0], own_sem.at[6])
    store.start()
    collect(0, PARTS - 1)

    store.wait()
    for copy in store_copies:
        copy.wait()
    for copy in fin_copies:
        copy.wait_recv()
    sent = list(raw_copies.values()) + key_copies + [weight_copies[1], weight_copies[3]] + [hidden_copy] + dh_copies
    sent += fin_copies + far_copies
    for unit in order[len(order) - OUTS :]:
        sent += x_copies[unit]
    for copies in ret_copies.values():
        sent += copies
    for copy in sent:
        copy.wait_send()


def last(own_ref, far_ref, weight_ref, in_grad, weight_grad, own, far, share, sems):
    rows, high = ROWS // 4, FFW // 4
    loads, stores = [], []
    for t in range(4):
        at, part = pl.ds(t * rows, rows), pl.ds(t * high, high)
        loads.append(
            [
                pltpu.make_async_copy(own_ref.at[at], own.at[at], sems.at[0, t]),
                pltpu.make_async_copy(far_ref.at[at], far.at[at], sems.at[1, t]),
                pltpu.make_async_copy(weight_ref.at[0, part], share.at[part], sems.at[2, t]),
            ]
        )
        stores.append(
            [
                pltpu.make_async_copy(own.at[at], in_grad.at[at], sems.at[3, t]),
                pltpu.make_async_copy(share.at[part], weight_grad.at[0, part], sems.at[4, t]),
            ]
        )
        for load in loads[t]:
            load.start()
    for t in range(4):
        at = pl.ds(t * rows, rows)
        for load in loads[t]:
            load.wait()
        own[at, :] = own[at, :] + far[at, :]
        for store in stores[t]:
            store.start()
    for group in stores:
        for store in group:
            store.wait()


def finish(own_grad, far_grad, weight_grad):
    hbm = pl.BlockSpec(memory_space=pl.ANY)
    return pl.pallas_call(
        last,
        out_shape=(
            jax.ShapeDtypeStruct(own_grad.shape, BF),
            jax.ShapeDtypeStruct(weight_grad.shape, BF),
        ),
        in_specs=[hbm, hbm, hbm],
        out_specs=(hbm, hbm),
        scratch_shapes=[
            pltpu.VMEM((ROWS, 2 * FFW), BF),
            pltpu.VMEM((ROWS, 2 * FFW), BF),
            pltpu.VMEM((FFW, FEAT), BF),
            pltpu.SemaphoreType.DMA((5, 4)),
        ],
        name="finish",
    )(own_grad, far_grad, weight_grad)


def shards(out_grad, expert_ids, stash_codes, stash_scale, down_weight):
    dma = pltpu.SemaphoreType.DMA
    hbm = pl.BlockSpec(memory_space=pl.ANY)
    vmem = pl.BlockSpec(memory_space=pltpu.VMEM)
    scratch = [
        pltpu.VMEM((4, 4, ROWS, FEAT), BF),
        pltpu.VMEM((4, ROWS, FEAT), BF),
        pltpu.VMEM((OUTS, HALF, FEAT), BF),
        pltpu.VMEM((4, 4, HALF, FEAT), BF),
        pltpu.VMEM((4, FFW, FEAT), BF),
        pltpu.VMEM((FFW, FEAT), BF),
        pltpu.VMEM((2, FFW // 2, FEAT), BF),
        pltpu.VMEM((FFW, 2 * SLOTS), BF),
        pltpu.VMEM((2, HALF, 2 * FFW), BF),
        pltpu.VMEM((4, HALF, FFW), F32),
        pltpu.VMEM((2, HALF, FFW), BF),
        pltpu.VMEM((2, HALF, FFW), BF),
        pltpu.VMEM((2, HALF, 2 * FFW), BF),
        pltpu.VMEM((2, HALF, 2 * FFW), BF),
        pltpu.VMEM((4, HALF, ROWS), BF),
        pltpu.VMEM((2, ROWS, HALF), BF),
        pltpu.VMEM((4, 8, ROWS), jnp.int32),
        pltpu.VMEM((2, ROWS, 2 * FFW), BF),
        pltpu.VMEM((16, 16, CAP), jnp.int32),
    ]
    for shape in [(4, 4), (4,), (4,), (16, 8), (1,), (2,), (2,), (2,), (2, PARTS, 8), (PARTS,)]:
        scratch += [dma(shape), dma(shape)]
    scratch += [dma((7,)), dma((4,)), dma((16,)), dma((2, PARTS)), dma((PARTS,)), dma((4,))]
    own_grad, far_grad, weight_grad, _ = pl.pallas_call(
        kernel,
        out_shape=(
            jax.ShapeDtypeStruct((ROWS, 2 * FFW), BF),
            jax.ShapeDtypeStruct((ROWS, 2 * FFW), BF),
            jax.ShapeDtypeStruct((1, FFW, FEAT), BF),
            jax.ShapeDtypeStruct((2, FFW, FEAT), BF),
        ),
        in_specs=[hbm, vmem, hbm, hbm, hbm],
        out_specs=(hbm, hbm, hbm, hbm),
        scratch_shapes=scratch,
        compiler_params=pltpu.CompilerParams(
            collective_id=0, has_side_effects=True, vmem_limit_bytes=60 * 2**20
        ),
        name="expert_backward",
    )(out_grad, expert_ids.reshape(1, ROWS), stash_codes, jnp.swapaxes(stash_scale, 3, 4), down_weight)
    return finish(own_grad, far_grad, weight_grad)


def solution(mesh):
    placed = (
        P(("expert", "fsdp"), None),
        P(("expert", "fsdp"), None),
        P("expert", "fsdp", None, None, None),
        P("expert", "fsdp", None, None, None),
        P("expert", None, "fsdp"),
    )
    return jax.shard_map(
        shards,
        mesh=mesh,
        in_specs=placed,
        out_specs=(P(("expert", "fsdp"), None), P("expert", None, "fsdp")),
        check_vma=False,
    )
```

```python
import jax
import jax.numpy as jnp
from jax import lax
from jax.experimental import pallas as pl
from jax.experimental.pallas import tpu as pltpu
from jax.sharding import PartitionSpec as P

FFW = 1024
BLOCK = 128
CAP = 48
ROWS = 256
FEAT = 896
HALF = 8 * CAP
SLOTS = 2 * HALF
OUTS = 6
PLACE = (0, 2, 1, 3)
ORDER = (2, 1, 3, 0)
PARTS = 4
PCOLS = 2 * FFW // PARTS
MESH = pl.DeviceIdType.MESH
BF = jnp.bfloat16
F32 = jnp.float32


def kernel(
    grad, ids, stash, scale_in, weight,
    own_grad, far_grad, weight_grad, parts,
    raw, merged, out, rows, wts, far_part, far_in, hidden, coef, dh, dh_out, dh_in, back, ret, pick, pick_t, keys, fin, scale,
    raw_s, raw_r, key_s, key_r, w_s, w_r, x_s, x_r, hid_s, hid_r, dh_s, dh_r, far_s, far_r, part_s, part_r, ret_s, ret_r, fin_s, fin_r,
    own_sem, other_sem, stash_sem, self_sem, store_sem, load_sem,
):
    e = lax.axis_index("expert")
    f = lax.axis_index("fsdp")
    zh, x, c = e // 8, (e // 2) % 4, e % 2
    zl, y = f // 4, f % 4

    def z_peer(d):
        h = 1 - zh if d & 2 else zh
        l = 1 - zl if d & 1 else zl
        return (h * 8 + x * 2 + c, l * 4 + y)

    def xc(k, sign):
        dx, dc = k // 2, k % 2
        return lax.rem(x + (4 + sign * dx), 4), (1 - c if dc else c)

    def x_peer(k, sign):
        px, pc = xc(k, sign)
        return (zh * 8 + px * 2 + pc, f)

    def y_peer(j):
        return (e, zl * 4 + lax.rem(y + 4 + j, 4))

    def remote(src, dst, s, r, device):
        return pltpu.make_async_remote_copy(
            src_ref=src, dst_ref=dst, send_sem=s, recv_sem=r, device_id=device, device_id_type=MESH
        )

    barrier = pltpu.get_barrier_semaphore()
    peers = [z_peer(d) for d in (1, 2, 3)] + [x_peer(k, 1) for k in range(1, 8)] + [y_peer(j) for j in (1, 2, 3)]
    for peer in peers:
        pl.semaphore_signal(barrier, inc=1, device_id=peer, device_id_type=MESH)

    def columns(half, j):
        quarter = lax.rem(y + j, 4)
        return pl.ds(pl.multiple_of((half * 4 + quarter) * FEAT, 128), FEAT)

    own_rows = {
        j: pltpu.make_async_copy(grad.at[:, columns(zl, j)], raw.at[0, j], own_sem.at[j]) for j in ORDER
    }
    other_rows = {
        j: pltpu.make_async_copy(grad.at[:, columns(1 - zl, j)], merged.at[j], other_sem.at[j]) for j in ORDER
    }
    stash_copies = [pltpu.make_async_copy(scale_in.at[0, 0], scale, own_sem.at[5])]
    for s in range(16):
        sx, sc = xc(s % 8, -1)
        g = (1 - zh if s // 8 else zh) * 8 + sx * 2 + sc
        stash_copies.append(
            pltpu.make_async_copy(stash.at[0, 0, g], back.at[s // 8, pl.ds((s % 8) * CAP, CAP)], stash_sem.at[s])
        )
    own_weight = pltpu.make_async_copy(weight.at[0], wts.at[0], own_sem.at[4])
    for j in ORDER:
        own_rows[j].start()
        other_rows[j].start()

    expert_of = ids[...]
    same = lax.broadcasted_iota(jnp.int32, (16, ROWS), 0) == expert_of
    chosen = jnp.where(same, 1.0, 0.0)
    earlier = jnp.where(
        lax.broadcasted_iota(jnp.int32, (ROWS, ROWS), 0) < lax.broadcasted_iota(jnp.int32, (ROWS, ROWS), 1), 1.0, 0.0
    )
    count = jnp.dot(chosen.astype(BF), earlier.astype(BF), preferred_element_type=F32)
    slot = jnp.sum(chosen * count, axis=0, keepdims=True)
    key = expert_of * CAP + slot.astype(jnp.int32)
    keys[0] = jnp.broadcast_to(key, (8, ROWS))

    place = lax.broadcasted_iota(jnp.int32, (CAP, ROWS), 0)

    def make_pick(d):
        key_of = keys[d, 0:1, :]
        for k in range(8):
            px, pc = xc(k, 1)
            base = (zh * 8 + px * 2 + pc) * CAP
            pick[d, k * CAP : (k + 1) * CAP, :] = jnp.where(key_of - base == place, 1.0, 0.0).astype(BF)

    make_pick(0)
    near = jnp.broadcast_to(expert_of // 8 == zh, (8, ROWS)).astype(F32).T[:, 0:1] > 0.5

    raw_copies = {}
    for j in ORDER:
        raw_copies[1, j] = remote(merged.at[j], raw.at[1, j], raw_s.at[1, j], raw_r.at[1, j], z_peer(1))
        raw_copies[2, j] = remote(raw.at[1, j], raw.at[2, j], raw_s.at[2, j], raw_r.at[2, j], z_peer(3))
        raw_copies[3, j] = remote(
            grad.at[:, columns(1 - zl, j)], raw.at[3, j], raw_s.at[3, j], raw_r.at[3, j], z_peer(3)
        )

    loaded = []

    def own_ready(j):
        if j not in loaded:
            loaded.append(j)
            own_rows[j].wait()

    def merge(j):
        other_rows[j].wait()
        own_ready(j)

        def tile(t, _):
            at = pl.ds(pl.multiple_of(t * BLOCK, BLOCK), BLOCK)
            merged[j, :, at] = jnp.where(near, merged[j, :, at].astype(F32), raw[0, j, :, at].astype(F32)).astype(BF)
            return 0

        lax.fori_loop(0, FEAT // BLOCK, tile, 0)
    key_copies = [remote(keys.at[0], keys.at[d], key_s.at[d], key_r.at[d], z_peer(d)) for d in (1, 2, 3)]
    weight_copies = {j: remote(weight.at[0], wts.at[j], w_s.at[j], w_r.at[j], y_peer(-j)) for j in (1, 3)}
    upper, lower = pl.ds(0, FFW // 2), pl.ds(FFW // 2, FFW // 2)
    weight_copies[0] = remote(wts.at[1, upper], wts.at[2, upper], w_s.at[0], w_r.at[0], y_peer(-1))
    weight_copies[2] = remote(wts.at[3, lower], wts.at[2, lower], w_s.at[2], w_r.at[2], y_peer(1))
    hidden_copy = remote(hidden.at[:, pl.ds(0, SLOTS)], hidden.at[:, pl.ds(SLOTS, SLOTS)], hid_s.at[0], hid_r.at[0], z_peer(1))
    dh_copies = [remote(dh_out.at[zr], dh_in.at[zr], dh_s.at[zr], dh_r.at[zr], z_peer(1)) for zr in range(2)]
    far_copies = [
        remote(far_part.at[half], far_in.at[n], far_s.at[n], far_r.at[n], y_peer(1 - 2 * n))
        for n, half in enumerate((upper, lower))
    ]
    part_copies = {
        j: remote(wts.at[j], parts.at[j // 2], part_s.at[j // 2], part_r.at[j // 2], y_peer(j)) for j in (1, 3)
    }

    x_copies = {}
    order = []

    def put(d, j):
        unit = len(order)
        into = unit % OUTS
        if unit >= OUTS:
            for copy in x_copies[order[unit - OUTS]]:
                copy.wait_send()
        order.append((d, j))
        if d:
            raw_copies[d, j].wait_recv()
        else:
            own_ready(j)
        if d == 1:
            raw_copies[2, j].start()

        def tile(t, _):
            at = pl.ds(pl.multiple_of(t * 192, 192), 192)
            out[into, at, :] = jnp.dot(pick[d, at, :], raw[d, j], preferred_element_type=F32).astype(BF)
            return 0

        lax.fori_loop(0, 2, tile, 0)
        rows[j, PLACE[d], 0:CAP, :] = out[into, 0:CAP, :]

    def dispatch(d, j):
        if (d, j) not in order:
            put(d, j)
        unit = order.index((d, j))
        into = unit % OUTS
        x_copies[d, j] = []
        for k in range(1, 8):
            block = pl.ds(k * CAP, CAP)
            copy = remote(
                out.at[into, block, :], rows.at[j, PLACE[d], block, :], x_s.at[unit, k], x_r.at[unit, k], x_peer(k, 1)
            )
            copy.start()
            x_copies[d, j].append(copy)

    def gate_tile(s, _):
        zr, k = s // 8, s % 8
        dx, dc = k // 2, k % 2
        sx = lax.rem(x + 4 - dx, 4)
        sc = c + dc - 2 * c * dc
        sz = zh + zr - 2 * zh * zr
        factor = jnp.exp2(scale[sz * 8 + sx * 2 + sc].astype(F32)).T
        at = pl.ds(pl.multiple_of(k * CAP, CAP), CAP)
        for b in range(FFW // BLOCK):
            low, high = slice(b * BLOCK, (b + 1) * BLOCK), slice(FFW + b * BLOCK, FFW + (b + 1) * BLOCK)
            gate = back[zr, at, low].astype(F32) * factor[:, b : b + 1]
            up = back[zr, at, high].astype(F32) * factor[:, 8 + b : 9 + b]
            sig = 1.0 / (1.0 + jnp.exp(-gate))
            silu = gate * sig
            dh_out[zr, at, low] = (silu * up).astype(BF)
            coef[zr, at, low] = (up * sig * (1.0 + gate * (1.0 - sig))).astype(BF)
            coef[zr, at, high] = silu.astype(BF)
        return 0

    def turn(b, _):
        at = pl.ds(pl.multiple_of(b * BLOCK, BLOCK), BLOCK)
        for zr in range(2):
            hidden[at, zr * HALF : (zr + 1) * HALF] = dh_out[zr, :, at].T
        return 0

    def arrived(j, sources):
        for d in sources:
            for copy in x_copies[d, j]:
                copy.wait_recv()

    def d_hidden(d, j):
        arrived(j, (d,))

        def tile(n, _):
            at = pl.ds(pl.multiple_of(n * 256, 256), 256)
            dh[PLACE[d], :, at] += lax.dot_general(
                rows[j, PLACE[d]], wts[j, at, :], (((1,), (1,)), ((), ())), preferred_element_type=F32
            )
            return 0

        lax.fori_loop(0, FFW // 256, tile, 0)

    def d_hidden_all(j, start):
        def tile(n, _):
            at = pl.ds(pl.multiple_of(n * 256, 256), 256)
            term = lax.dot_general(
                rows[j].reshape(2 * SLOTS, FEAT), wts[j, at, :], (((1,), (1,)), ((), ())), preferred_element_type=F32
            ).reshape(4, HALF, 256)
            dh[:, :, at] = term if start else dh[:, :, at] + term
            return 0

        lax.fori_loop(0, FFW // 256, tile, 0)

    def partial(j):
        into = far_part if j == 2 else wts.at[j]
        for n in range(2):

            def tile(m, _, n=n):
                at = pl.ds(pl.multiple_of(n * (FFW // 2) + m * 256, 256), 256)
                term = jnp.dot(hidden[at, :], rows[j].reshape(2 * SLOTS, FEAT), preferred_element_type=F32)
                if j == 1 + 2 * n:
                    term += far_in[n, pl.ds(pl.multiple_of(m * 256, 256), 256), :].astype(F32)
                into[at, :] = term.astype(BF)
                return 0

            if j == 1 + 2 * n:
                far_copies[n].wait_recv()
            lax.fori_loop(0, 2, tile, 0)
            if j == 2:
                far_copies[n].start()
        if j in (1, 3):
            part_copies[j].start()

    def exchange(zr):
        dh_out[zr] = dh[PLACE[1 + 2 * zr]].astype(BF)
        dh_copies[zr].start()

    ret_copies, self_copies, fin_copies, store_copies = {}, {}, [], []

    def send_back(zr):
        dh_copies[zr].wait_recv()
        for p in range(PARTS):
            cols = pl.ds(p * PCOLS, PCOLS)
            dh_cols = pl.ds((p * PCOLS) % FFW, PCOLS)

            def back_tile(k, _, cols=cols, dh_cols=dh_cols):
                at = pl.ds(pl.multiple_of(k * CAP, CAP), CAP)
                total = dh[PLACE[2 * zr], at, dh_cols] + dh_in[zr, at, dh_cols].astype(F32)
                back[zr, at, cols] = (total * coef[zr, at, cols].astype(F32)).astype(BF)
                return 0

            lax.fori_loop(0, 8, back_tile, 0)
            here = pltpu.make_async_copy(
                back.at[zr, pl.ds(0, CAP), cols], ret.at[zr, pl.ds(0, CAP), cols], self_sem.at[zr, p]
            )
            here.start()
            self_copies[zr, p] = here
            ret_copies[zr, p] = []
            for k in range(1, 8):
                block = pl.ds(k * CAP, CAP)
                copy = remote(
                    back.at[zr, block, cols], ret.at[zr, block, cols],
                    ret_s.at[zr, p, k], ret_r.at[zr, p, k], x_peer(k, -1),
                )
                copy.start()
                ret_copies[zr, p].append(copy)

    def collect(zr, p):
        cols = pl.ds(p * PCOLS, PCOLS)
        self_copies[zr, p].wait()
        for copy in ret_copies[zr, p]:
            copy.wait_recv()
        fin[zr, :, cols] = jnp.dot(pick_t[zr], ret[zr, :, cols], preferred_element_type=F32).astype(BF)
        if zr:
            copy = remote(fin.at[1, :, cols], far_grad.at[:, cols], fin_s.at[p], fin_r.at[p], z_peer(2))
            fin_copies.append(copy)
        else:
            copy = pltpu.make_async_copy(fin.at[0, :, cols], own_grad.at[:, cols], store_sem.at[p])
            store_copies.append(copy)
        copy.start()

    def collect_part(j):
        part_copies[j].wait_recv()
        part_copies[j].wait_send()
        load = pltpu.make_async_copy(parts.at[j // 2], wts.at[j], load_sem.at[j])
        load.start()
        return load

    a, b, g, o = ORDER
    put(0, a)
    pl.semaphore_wait(barrier, len(peers))
    dispatch(0, a)
    raw_copies[3, a].start()
    for copy in key_copies:
        copy.start()
    merge(a)
    raw_copies[1, a].start()
    weight_copies[1].start()
    weight_copies[3].start()
    merge(b)
    raw_copies[1, b].start()
    raw_copies[3, b].start()
    dispatch(0, b)
    dispatch(0, g)
    for copy in stash_copies:
        copy.start()
    merge(g)
    merge(o)
    own_weight.start()
    for copy in key_copies:
        copy.wait_recv()
    for d in (1, 3, 2):
        make_pick(d)
    for copy in stash_copies:
        copy.wait()
    lax.fori_loop(0, 16, gate_tile, 0)
    dispatch(1, a)
    dispatch(3, a)
    raw_copies[3, g].start()
    lax.fori_loop(0, FFW // BLOCK, turn, 0)
    hidden_copy.start()
    for n, d in enumerate((0, 2)):
        pick_t[n] = pick[d].astype(F32).T.astype(BF)
    dispatch(2, a)
    dispatch(1, b)
    dispatch(3, b)
    raw_copies[3, o].start()
    dispatch(2, b)
    raw_copies[1, g].start()
    weight_copies[1].wait_recv()
    weight_copies[0].start()
    weight_copies[3].wait_recv()
    weight_copies[2].start()
    dispatch(3, g)
    dispatch(3, o)
    raw_copies[1, o].start()
    arrived(a, (0, 1, 3, 2))
    hidden_copy.wait_recv()
    partial(a)
    dispatch(1, g)
    arrived(b, (0, 1, 3, 2))
    d_hidden_all(b, True)
    dispatch(2, g)
    weight_copies[0].wait_recv()
    weight_copies[2].wait_recv()
    d_hidden_all(a, False)
    own_weight.wait()
    d_hidden(3, g)
    d_hidden(3, o)
    exchange(1)
    dispatch(1, o)
    dispatch(2, o)
    dispatch(0, o)
    weight_copies[0].wait_send()
    partial(b)
    d_hidden(0, g)
    d_hidden(1, g)
    d_hidden(2, g)
    weight_copies[2].wait_send()
    partial(g)
    d_hidden(1, o)
    exchange(0)
    d_hidden(2, o)
    send_back(1)
    d_hidden(0, o)
    collect(1, 0)
    send_back(0)
    partial(o)
    for p in range(1, PARTS):
        collect(1, p)
    for p in range(PARTS - 1):
        collect(0, p)
    loads = [collect_part(b), collect_part(g)]
    for load in loads:
        load.wait()

    def sum_tile(t, _):
        at = pl.ds(pl.multiple_of(t * 64, 64), 64)
        total = wts[0, at, :].astype(F32)
        for j in (1, 3):
            total += wts[j, at, :].astype(F32)
        wts[0, at, :] = total.astype(BF)
        return 0

    lax.fori_loop(0, FFW // 64, sum_tile, 0)
    store = pltpu.make_async_copy(wts.at[0], weight_grad.at[0], own_sem.at[6])
    store.start()
    collect(0, PARTS - 1)

    store.wait()
    for copy in store_copies:
        copy.wait()
    for copy in fin_copies:
        copy.wait_recv()
    sent = list(raw_copies.values()) + key_copies + [weight_copies[1], weight_copies[3]] + [hidden_copy] + dh_copies
    sent += fin_copies + far_copies
    for unit in order[len(order) - OUTS :]:
        sent += x_copies[unit]
    for copies in ret_copies.values():
        sent += copies
    for copy in sent:
        copy.wait_send()


def last(own_ref, far_ref, weight_ref, in_grad, weight_grad, own, far, share, sems):
    rows, high = ROWS // 4, FFW // 4
    loads, stores = [], []
    for t in range(4):
        at, part = pl.ds(t * rows, rows), pl.ds(t * high, high)
        loads.append(
            [
                pltpu.make_async_copy(own_ref.at[at], own.at[at], sems.at[0, t]),
                pltpu.make_async_copy(far_ref.at[at], far.at[at], sems.at[1, t]),
                pltpu.make_async_copy(weight_ref.at[0, part], share.at[part], sems.at[2, t]),
            ]
        )
        stores.append(
            [
                pltpu.make_async_copy(own.at[at], in_grad.at[at], sems.at[3, t]),
                pltpu.make_async_copy(share.at[part], weight_grad.at[0, part], sems.at[4, t]),
            ]
        )
        for load in loads[t]:
            load.start()
    for t in range(4):
        at = pl.ds(t * rows, rows)
        for load in loads[t]:
            load.wait()
        own[at, :] = own[at, :] + far[at, :]
        for store in stores[t]:
            store.start()
    for group in stores:
        for store in group:
            store.wait()


def finish(own_grad, far_grad, weight_grad):
    hbm = pl.BlockSpec(memory_space=pl.ANY)
    return pl.pallas_call(
        last,
        out_shape=(
            jax.ShapeDtypeStruct(own_grad.shape, BF),
            jax.ShapeDtypeStruct(weight_grad.shape, BF),
        ),
        in_specs=[hbm, hbm, hbm],
        out_specs=(hbm, hbm),
        scratch_shapes=[
            pltpu.VMEM((ROWS, 2 * FFW), BF),
            pltpu.VMEM((ROWS, 2 * FFW), BF),
            pltpu.VMEM((FFW, FEAT), BF),
            pltpu.SemaphoreType.DMA((5, 4)),
        ],
        name="finish",
    )(own_grad, far_grad, weight_grad)


def shards(out_grad, expert_ids, stash_codes, stash_scale, down_weight):
    dma = pltpu.SemaphoreType.DMA
    hbm = pl.BlockSpec(memory_space=pl.ANY)
    vmem = pl.BlockSpec(memory_space=pltpu.VMEM)
    scratch = [
        pltpu.VMEM((4, 4, ROWS, FEAT), BF),
        pltpu.VMEM((4, ROWS, FEAT), BF),
        pltpu.VMEM((OUTS, HALF, FEAT), BF),
        pltpu.VMEM((4, 4, HALF, FEAT), BF),
        pltpu.VMEM((4, FFW, FEAT), BF),
        pltpu.VMEM((FFW, FEAT), BF),
        pltpu.VMEM((2, FFW // 2, FEAT), BF),
        pltpu.VMEM((FFW, 2 * SLOTS), BF),
        pltpu.VMEM((2, HALF, 2 * FFW), BF),
        pltpu.VMEM((4, HALF, FFW), F32),
        pltpu.VMEM((2, HALF, FFW), BF),
        pltpu.VMEM((2, HALF, FFW), BF),
        pltpu.VMEM((2, HALF, 2 * FFW), BF),
        pltpu.VMEM((2, HALF, 2 * FFW), BF),
        pltpu.VMEM((4, HALF, ROWS), BF),
        pltpu.VMEM((2, ROWS, HALF), BF),
        pltpu.VMEM((4, 8, ROWS), jnp.int32),
        pltpu.VMEM((2, ROWS, 2 * FFW), BF),
        pltpu.VMEM((16, 16, CAP), jnp.int32),
    ]
    for shape in [(4, 4), (4,), (4,), (16, 8), (1,), (2,), (2,), (2,), (2, PARTS, 8), (PARTS,)]:
        scratch += [dma(shape), dma(shape)]
    scratch += [dma((7,)), dma((4,)), dma((16,)), dma((2, PARTS)), dma((PARTS,)), dma((4,))]
    own_grad, far_grad, weight_grad, _ = pl.pallas_call(
        kernel,
        out_shape=(
            jax.ShapeDtypeStruct((ROWS, 2 * FFW), BF),
            jax.ShapeDtypeStruct((ROWS, 2 * FFW), BF),
            jax.ShapeDtypeStruct((1, FFW, FEAT), BF),
            jax.ShapeDtypeStruct((2, FFW, FEAT), BF),
        ),
        in_specs=[hbm, vmem, hbm, hbm, hbm],
        out_specs=(hbm, hbm, hbm, hbm),
        scratch_shapes=scratch,
        compiler_params=pltpu.CompilerParams(
            collective_id=0, has_side_effects=True, vmem_limit_bytes=60 * 2**20
        ),
        name="expert_backward",
    )(out_grad, expert_ids.reshape(1, ROWS), stash_codes, jnp.swapaxes(stash_scale, 3, 4), down_weight)
    return finish(own_grad, far_grad, weight_grad)


def solution(mesh):
    placed = (
        P(("expert", "fsdp"), None),
        P(("expert", "fsdp"), None),
        P("expert", "fsdp", None, None, None),
        P("expert", "fsdp", None, None, None),
        P("expert", None, "fsdp"),
    )
    return jax.shard_map(
        shards,
        mesh=mesh,
        in_specs=placed,
        out_specs=(P(("expert", "fsdp"), None), P("expert", None, "fsdp")),
        check_vma=False,
    )
```

```python
import jax
import jax.numpy as jnp
from jax import lax
from jax.experimental import pallas as pl
from jax.experimental.pallas import tpu as pltpu
from jax.sharding import PartitionSpec as P

FFW = 1024
BLOCK = 128
CAP = 48
ROWS = 256
FEAT = 896
HALF = 8 * CAP
SLOTS = 2 * HALF
OUTS = 6
PLACE = (0, 2, 1, 3)
ORDER = (2, 1, 3, 0)
PARTS = 4
PCOLS = 2 * FFW // PARTS
MESH = pl.DeviceIdType.MESH
BF = jnp.bfloat16
F32 = jnp.float32


def kernel(
    grad, ids, stash, scale_in, weight,
    own_grad, far_grad, weight_grad, parts,
    raw, merged, out, rows, wts, far_part, far_in, hidden, coef, dh, dh_out, dh_in, back, ret, pick, pick_t, keys, fin, scale,
    raw_s, raw_r, key_s, key_r, w_s, w_r, x_s, x_r, hid_s, hid_r, dh_s, dh_r, far_s, far_r, part_s, part_r, ret_s, ret_r, fin_s, fin_r,
    own_sem, other_sem, stash_sem, self_sem, load_sem,
):
    e = lax.axis_index("expert")
    f = lax.axis_index("fsdp")
    zh, x, c = e // 8, (e // 2) % 4, e % 2
    zl, y = f // 4, f % 4

    def z_peer(d):
        h = 1 - zh if d & 2 else zh
        l = 1 - zl if d & 1 else zl
        return (h * 8 + x * 2 + c, l * 4 + y)

    def xc(k, sign):
        dx, dc = k // 2, k % 2
        return lax.rem(x + (4 + sign * dx), 4), (1 - c if dc else c)

    def x_peer(k, sign):
        px, pc = xc(k, sign)
        return (zh * 8 + px * 2 + pc, f)

    def y_peer(j):
        return (e, zl * 4 + lax.rem(y + 4 + j, 4))

    def remote(src, dst, s, r, device):
        return pltpu.make_async_remote_copy(
            src_ref=src, dst_ref=dst, send_sem=s, recv_sem=r, device_id=device, device_id_type=MESH
        )

    barrier = pltpu.get_barrier_semaphore()
    peers = [z_peer(d) for d in (1, 2, 3)] + [x_peer(k, 1) for k in range(1, 8)] + [y_peer(j) for j in (1, 2, 3)]
    for peer in peers:
        pl.semaphore_signal(barrier, inc=1, device_id=peer, device_id_type=MESH)

    def columns(half, j):
        quarter = lax.rem(y + j, 4)
        return pl.ds(pl.multiple_of((half * 4 + quarter) * FEAT, 128), FEAT)

    own_rows = {
        j: pltpu.make_async_copy(grad.at[:, columns(zl, j)], raw.at[0, j], own_sem.at[j]) for j in ORDER
    }
    other_rows = {
        j: pltpu.make_async_copy(grad.at[:, columns(1 - zl, j)], merged.at[j], other_sem.at[j]) for j in ORDER
    }
    stash_copies = [pltpu.make_async_copy(scale_in.at[0, 0], scale, own_sem.at[5])]
    for s in range(16):
        sx, sc = xc(s % 8, -1)
        g = (1 - zh if s // 8 else zh) * 8 + sx * 2 + sc
        stash_copies.append(
            pltpu.make_async_copy(stash.at[0, 0, g], back.at[s // 8, pl.ds((s % 8) * CAP, CAP)], stash_sem.at[s])
        )
    own_weight = pltpu.make_async_copy(weight.at[0], wts.at[0], own_sem.at[4])
    for j in ORDER:
        own_rows[j].start()
        other_rows[j].start()

    expert_of = ids[...]
    same = lax.broadcasted_iota(jnp.int32, (16, ROWS), 0) == expert_of
    chosen = jnp.where(same, 1.0, 0.0)
    earlier = jnp.where(
        lax.broadcasted_iota(jnp.int32, (ROWS, ROWS), 0) < lax.broadcasted_iota(jnp.int32, (ROWS, ROWS), 1), 1.0, 0.0
    )
    count = jnp.dot(chosen.astype(BF), earlier.astype(BF), preferred_element_type=F32)
    slot = jnp.sum(chosen * count, axis=0, keepdims=True)
    key = expert_of * CAP + slot.astype(jnp.int32)
    keys[0] = jnp.broadcast_to(key, (8, ROWS))

    place = lax.broadcasted_iota(jnp.int32, (CAP, ROWS), 0)

    def make_pick(d):
        key_of = keys[d, 0:1, :]
        for k in range(8):
            px, pc = xc(k, 1)
            base = (zh * 8 + px * 2 + pc) * CAP
            pick[d, k * CAP : (k + 1) * CAP, :] = jnp.where(key_of - base == place, 1.0, 0.0).astype(BF)

    make_pick(0)
    near = jnp.broadcast_to(expert_of // 8 == zh, (8, ROWS)).astype(F32).T[:, 0:1] > 0.5

    raw_copies = {}
    for j in ORDER:
        raw_copies[1, j] = remote(merged.at[j], raw.at[1, j], raw_s.at[1, j], raw_r.at[1, j], z_peer(1))
        raw_copies[2, j] = remote(raw.at[1, j], raw.at[2, j], raw_s.at[2, j], raw_r.at[2, j], z_peer(3))
        raw_copies[3, j] = remote(
            grad.at[:, columns(1 - zl, j)], raw.at[3, j], raw_s.at[3, j], raw_r.at[3, j], z_peer(3)
        )

    loaded = []

    def own_ready(j):
        if j not in loaded:
            loaded.append(j)
            own_rows[j].wait()

    def merge(j):
        other_rows[j].wait()
        own_ready(j)

        def tile(t, _):
            at = pl.ds(pl.multiple_of(t * BLOCK, BLOCK), BLOCK)
            merged[j, :, at] = jnp.where(near, merged[j, :, at].astype(F32), raw[0, j, :, at].astype(F32)).astype(BF)
            return 0

        lax.fori_loop(0, FEAT // BLOCK, tile, 0)
    key_copies = [remote(keys.at[0], keys.at[d], key_s.at[d], key_r.at[d], z_peer(d)) for d in (1, 2, 3)]
    weight_copies = {j: remote(weight.at[0], wts.at[j], w_s.at[j], w_r.at[j], y_peer(-j)) for j in (1, 3)}
    upper, lower = pl.ds(0, FFW // 2), pl.ds(FFW // 2, FFW // 2)
    weight_copies[0] = remote(wts.at[1, upper], wts.at[2, upper], w_s.at[0], w_r.at[0], y_peer(-1))
    weight_copies[2] = remote(wts.at[3, lower], wts.at[2, lower], w_s.at[2], w_r.at[2], y_peer(1))
    hidden_copy = remote(hidden.at[:, pl.ds(0, SLOTS)], hidden.at[:, pl.ds(SLOTS, SLOTS)], hid_s.at[0], hid_r.at[0], z_peer(1))
    dh_copies = [remote(dh_out.at[zr], dh_in.at[zr], dh_s.at[zr], dh_r.at[zr], z_peer(1)) for zr in range(2)]
    far_copies = [
        remote(far_part.at[half], far_in.at[n], far_s.at[n], far_r.at[n], y_peer(1 - 2 * n))
        for n, half in enumerate((upper, lower))
    ]
    part_copies = {
        j: remote(wts.at[j], parts.at[j // 2], part_s.at[j // 2], part_r.at[j // 2], y_peer(j)) for j in (1, 3)
    }

    x_copies = {}
    order = []

    def put(d, j):
        unit = len(order)
        into = unit % OUTS
        if unit >= OUTS:
            for copy in x_copies[order[unit - OUTS]]:
                copy.wait_send()
        order.append((d, j))
        if d:
            raw_copies[d, j].wait_recv()
        else:
            own_ready(j)
        if d == 1:
            raw_copies[2, j].start()

        def tile(t, _):
            at = pl.ds(pl.multiple_of(t * 192, 192), 192)
            out[into, at, :] = jnp.dot(pick[d, at, :], raw[d, j], preferred_element_type=F32).astype(BF)
            return 0

        lax.fori_loop(0, 2, tile, 0)
        rows[j, PLACE[d], 0:CAP, :] = out[into, 0:CAP, :]

    def dispatch(d, j):
        if (d, j) not in order:
            put(d, j)
        unit = order.index((d, j))
        into = unit % OUTS
        x_copies[d, j] = []
        for k in range(1, 8):
            block = pl.ds(k * CAP, CAP)
            copy = remote(
                out.at[into, block, :], rows.at[j, PLACE[d], block, :], x_s.at[unit, k], x_r.at[unit, k], x_peer(k, 1)
            )
            copy.start()
            x_copies[d, j].append(copy)

    def gate_tile(s, _):
        zr, k = s // 8, s % 8
        dx, dc = k // 2, k % 2
        sx = lax.rem(x + 4 - dx, 4)
        sc = c + dc - 2 * c * dc
        sz = zh + zr - 2 * zh * zr
        factor = jnp.exp2(scale[sz * 8 + sx * 2 + sc].astype(F32)).T
        at = pl.ds(pl.multiple_of(k * CAP, CAP), CAP)
        for b in range(FFW // BLOCK):
            low, high = slice(b * BLOCK, (b + 1) * BLOCK), slice(FFW + b * BLOCK, FFW + (b + 1) * BLOCK)
            gate = back[zr, at, low].astype(F32) * factor[:, b : b + 1]
            up = back[zr, at, high].astype(F32) * factor[:, 8 + b : 9 + b]
            sig = 1.0 / (1.0 + jnp.exp(-gate))
            silu = gate * sig
            dh_out[zr, at, low] = (silu * up).astype(BF)
            coef[zr, at, low] = (up * sig * (1.0 + gate * (1.0 - sig))).astype(BF)
            coef[zr, at, high] = silu.astype(BF)
        return 0

    def turn(b, _):
        at = pl.ds(pl.multiple_of(b * BLOCK, BLOCK), BLOCK)
        for zr in range(2):
            hidden[at, zr * HALF : (zr + 1) * HALF] = dh_out[zr, :, at].T
        return 0

    def arrived(j, sources):
        for d in sources:
            for copy in x_copies[d, j]:
                copy.wait_recv()

    def d_hidden(d, j):
        arrived(j, (d,))

        def tile(n, _):
            at = pl.ds(pl.multiple_of(n * 256, 256), 256)
            dh[PLACE[d], :, at] += lax.dot_general(
                rows[j, PLACE[d]], wts[j, at, :], (((1,), (1,)), ((), ())), preferred_element_type=F32
            )
            return 0

        lax.fori_loop(0, FFW // 256, tile, 0)

    def d_hidden_all(j, start):
        def tile(n, _):
            at = pl.ds(pl.multiple_of(n * 256, 256), 256)
            term = lax.dot_general(
                rows[j].reshape(2 * SLOTS, FEAT), wts[j, at, :], (((1,), (1,)), ((), ())), preferred_element_type=F32
            ).reshape(4, HALF, 256)
            dh[:, :, at] = term if start else dh[:, :, at] + term
            return 0

        lax.fori_loop(0, FFW // 256, tile, 0)

    def partial(j):
        into = far_part if j == 2 else wts.at[j]
        for n in range(2):

            def tile(m, _, n=n):
                at = pl.ds(pl.multiple_of(n * (FFW // 2) + m * 256, 256), 256)
                term = jnp.dot(hidden[at, :], rows[j].reshape(2 * SLOTS, FEAT), preferred_element_type=F32)
                if j == 1 + 2 * n:
                    term += far_in[n, pl.ds(pl.multiple_of(m * 256, 256), 256), :].astype(F32)
                into[at, :] = term.astype(BF)
                return 0

            if j == 1 + 2 * n:
                far_copies[n].wait_recv()
            lax.fori_loop(0, 2, tile, 0)
            if j == 2:
                far_copies[n].start()
        if j in (1, 3):
            part_copies[j].start()

    def exchange(zr):
        dh_out[zr] = dh[PLACE[1 + 2 * zr]].astype(BF)
        dh_copies[zr].start()

    ret_copies, self_copies, fin_copies = {}, {}, []

    def send_back(zr):
        dh_copies[zr].wait_recv()
        for p in range(PARTS):
            cols = pl.ds(p * PCOLS, PCOLS)
            dh_cols = pl.ds((p * PCOLS) % FFW, PCOLS)

            def back_tile(k, _, cols=cols, dh_cols=dh_cols):
                at = pl.ds(pl.multiple_of(k * CAP, CAP), CAP)
                total = dh[PLACE[2 * zr], at, dh_cols] + dh_in[zr, at, dh_cols].astype(F32)
                back[zr, at, cols] = (total * coef[zr, at, cols].astype(F32)).astype(BF)
                return 0

            lax.fori_loop(0, 8, back_tile, 0)
            here = pltpu.make_async_copy(
                back.at[zr, pl.ds(0, CAP), cols], ret.at[zr, pl.ds(0, CAP), cols], self_sem.at[zr, p]
            )
            here.start()
            self_copies[zr, p] = here
            ret_copies[zr, p] = []
            for k in range(1, 8):
                block = pl.ds(k * CAP, CAP)
                copy = remote(
                    back.at[zr, block, cols], ret.at[zr, block, cols],
                    ret_s.at[zr, p, k], ret_r.at[zr, p, k], x_peer(k, -1),
                )
                copy.start()
                ret_copies[zr, p].append(copy)

    def collect(zr, p):
        cols = pl.ds(p * PCOLS, PCOLS)
        self_copies[zr, p].wait()
        for copy in ret_copies[zr, p]:
            copy.wait_recv()
        got = jnp.dot(pick_t[zr], ret[zr, :, cols], preferred_element_type=F32).astype(BF)
        if zr:
            fin[:, cols] = got
            copy = remote(fin.at[:, cols], far_grad.at[:, cols], fin_s.at[p], fin_r.at[p], z_peer(2))
            copy.start()
            fin_copies.append(copy)
        else:
            own_grad[:, cols] = got

    def collect_part(j):
        part_copies[j].wait_recv()
        part_copies[j].wait_send()
        load = pltpu.make_async_copy(parts.at[j // 2], wts.at[j], load_sem.at[j])
        load.start()
        return load

    a, b, g, o = ORDER
    put(0, a)
    pl.semaphore_wait(barrier, len(peers))
    dispatch(0, a)
    raw_copies[3, a].start()
    for copy in key_copies:
        copy.start()
    merge(a)
    raw_copies[1, a].start()
    weight_copies[1].start()
    weight_copies[3].start()
    merge(b)
    raw_copies[1, b].start()
    raw_copies[3, b].start()
    dispatch(0, b)
    dispatch(0, g)
    for copy in stash_copies:
        copy.start()
    merge(g)
    merge(o)
    own_weight.start()
    for copy in key_copies:
        copy.wait_recv()
    for d in (1, 3, 2):
        make_pick(d)
    for copy in stash_copies:
        copy.wait()
    lax.fori_loop(0, 16, gate_tile, 0)
    dispatch(1, a)
    dispatch(3, a)
    raw_copies[3, g].start()
    lax.fori_loop(0, FFW // BLOCK, turn, 0)
    hidden_copy.start()
    for n, d in enumerate((0, 2)):
        pick_t[n] = pick[d].astype(F32).T.astype(BF)
    dispatch(2, a)
    dispatch(1, b)
    dispatch(3, b)
    raw_copies[3, o].start()
    dispatch(2, b)
    raw_copies[1, g].start()
    weight_copies[1].wait_recv()
    weight_copies[0].start()
    weight_copies[3].wait_recv()
    weight_copies[2].start()
    dispatch(3, g)
    dispatch(3, o)
    raw_copies[1, o].start()
    arrived(a, (0, 1, 3, 2))
    hidden_copy.wait_recv()
    partial(a)
    dispatch(1, g)
    arrived(b, (0, 1, 3, 2))
    d_hidden_all(b, True)
    dispatch(2, g)
    weight_copies[0].wait_recv()
    weight_copies[2].wait_recv()
    d_hidden_all(a, False)
    own_weight.wait()
    d_hidden(3, g)
    d_hidden(3, o)
    exchange(1)
    dispatch(1, o)
    dispatch(2, o)
    dispatch(0, o)
    weight_copies[0].wait_send()
    partial(b)
    d_hidden(0, g)
    d_hidden(1, g)
    d_hidden(2, g)
    weight_copies[2].wait_send()
    partial(g)
    d_hidden(1, o)
    exchange(0)
    d_hidden(2, o)
    send_back(1)
    d_hidden(0, o)
    collect(1, 0)
    send_back(0)
    partial(o)
    for p in range(1, PARTS):
        collect(1, p)
    for p in range(PARTS - 1):
        collect(0, p)
    loads = [collect_part(b), collect_part(g)]
    for load in loads:
        load.wait()

    def sum_tile(t, _):
        at = pl.ds(pl.multiple_of(t * 64, 64), 64)
        total = wts[0, at, :].astype(F32)
        for j in (1, 3):
            total += wts[j, at, :].astype(F32)
        weight_grad[0, at, :] = total.astype(BF)
        return 0

    lax.fori_loop(0, FFW // 64, sum_tile, 0)
    collect(0, PARTS - 1)
    for copy in fin_copies:
        copy.wait_recv()
    sent = list(raw_copies.values()) + key_copies + [weight_copies[1], weight_copies[3]] + [hidden_copy] + dh_copies
    sent += fin_copies + far_copies
    for unit in order[len(order) - OUTS :]:
        sent += x_copies[unit]
    for copies in ret_copies.values():
        sent += copies
    for copy in sent:
        copy.wait_send()


def last(own, far, share, in_grad, weight_grad, total, sems):
    rows = ROWS // 4
    out = pltpu.make_async_copy(share, weight_grad, sems.at[4])
    out.start()
    stores = []
    for t in range(4):
        at = pl.ds(t * rows, rows)
        total[at, :] = own[at, :] + far[at, :]
        store = pltpu.make_async_copy(total.at[at], in_grad.at[at], sems.at[t])
        store.start()
        stores.append(store)
    for store in stores:
        store.wait()
    out.wait()


def finish(own_grad, far_grad, weight_grad):
    hbm = pl.BlockSpec(memory_space=pl.ANY)
    vmem = pl.BlockSpec(memory_space=pltpu.VMEM)
    return pl.pallas_call(
        last,
        out_shape=(
            jax.ShapeDtypeStruct(own_grad.shape, BF),
            jax.ShapeDtypeStruct(weight_grad.shape, BF),
        ),
        in_specs=[vmem, vmem, vmem],
        out_specs=(hbm, hbm),
        scratch_shapes=[
            pltpu.VMEM((ROWS, 2 * FFW), BF),
            pltpu.SemaphoreType.DMA((5,)),
        ],
        compiler_params=pltpu.CompilerParams(vmem_limit_bytes=8 * 2**20),
        name="finish",
    )(own_grad, far_grad, weight_grad)


def shards(out_grad, expert_ids, stash_codes, stash_scale, down_weight):
    dma = pltpu.SemaphoreType.DMA
    hbm = pl.BlockSpec(memory_space=pl.ANY)
    vmem = pl.BlockSpec(memory_space=pltpu.VMEM)
    scratch = [
        pltpu.VMEM((4, 4, ROWS, FEAT), BF),
        pltpu.VMEM((4, ROWS, FEAT), BF),
        pltpu.VMEM((OUTS, HALF, FEAT), BF),
        pltpu.VMEM((4, 4, HALF, FEAT), BF),
        pltpu.VMEM((4, FFW, FEAT), BF),
        pltpu.VMEM((FFW, FEAT), BF),
        pltpu.VMEM((2, FFW // 2, FEAT), BF),
        pltpu.VMEM((FFW, 2 * SLOTS), BF),
        pltpu.VMEM((2, HALF, 2 * FFW), BF),
        pltpu.VMEM((4, HALF, FFW), F32),
        pltpu.VMEM((2, HALF, FFW), BF),
        pltpu.VMEM((2, HALF, FFW), BF),
        pltpu.VMEM((2, HALF, 2 * FFW), BF),
        pltpu.VMEM((2, HALF, 2 * FFW), BF),
        pltpu.VMEM((4, HALF, ROWS), BF),
        pltpu.VMEM((2, ROWS, HALF), BF),
        pltpu.VMEM((4, 8, ROWS), jnp.int32),
        pltpu.VMEM((ROWS, 2 * FFW), BF),
        pltpu.VMEM((16, 16, CAP), jnp.int32),
    ]
    for shape in [(4, 4), (4,), (4,), (16, 8), (1,), (2,), (2,), (2,), (2, PARTS, 8), (PARTS,)]:
        scratch += [dma(shape), dma(shape)]
    scratch += [dma((6,)), dma((4,)), dma((16,)), dma((2, PARTS)), dma((4,))]
    own_grad, far_grad, weight_grad, _ = pl.pallas_call(
        kernel,
        out_shape=(
            pltpu.VMEM((ROWS, 2 * FFW), BF),
            pltpu.VMEM((ROWS, 2 * FFW), BF),
            pltpu.VMEM((1, FFW, FEAT), BF),
            jax.ShapeDtypeStruct((2, FFW, FEAT), BF),
        ),
        in_specs=[hbm, vmem, hbm, hbm, hbm],
        out_specs=(vmem, vmem, vmem, hbm),
        scratch_shapes=scratch,
        compiler_params=pltpu.CompilerParams(
            collective_id=0, has_side_effects=True, vmem_limit_bytes=58 * 2**20
        ),
        name="expert_backward",
    )(out_grad, expert_ids.reshape(1, ROWS), stash_codes, jnp.swapaxes(stash_scale, 3, 4), down_weight)
    return finish(own_grad, far_grad, weight_grad)


def solution(mesh):
    placed = (
        P(("expert", "fsdp"), None),
        P(("expert", "fsdp"), None),
        P("expert", "fsdp", None, None, None),
        P("expert", "fsdp", None, None, None),
        P("expert", None, "fsdp"),
    )
    return jax.shard_map(
        shards,
        mesh=mesh,
        in_specs=placed,
        out_specs=(P(("expert", "fsdp"), None), P("expert", None, "fsdp")),
        check_vma=False,
    )
```

```python
import jax
import jax.numpy as jnp
from jax import lax
from jax.experimental import pallas as pl
from jax.experimental.pallas import tpu as pltpu
from jax.sharding import PartitionSpec as P

FFW = 1024
BLOCK = 128
CAP = 48
ROWS = 256
FEAT = 896
HALF = 8 * CAP
SLOTS = 2 * HALF
OUTS = 6
PLACE = (0, 2, 1, 3)
ORDER = (2, 1, 3, 0)
PARTS = 4
PCOLS = 2 * FFW // PARTS
MESH = pl.DeviceIdType.MESH
BF = jnp.bfloat16
F32 = jnp.float32


def kernel(
    grad, ids, stash, scale_in, weight,
    own_grad, far_grad, weight_grad, parts,
    raw, merged, out, rows, wts, far_part, far_in, hidden, coef, dh, dh_out, dh_in, back, ret, pick, pick_t, keys, fin, scale,
    raw_s, raw_r, key_s, key_r, w_s, w_r, x_s, x_r, hid_s, hid_r, dh_s, dh_r, far_s, far_r, part_s, part_r, ret_s, ret_r, fin_s, fin_r,
    own_sem, other_sem, stash_sem, self_sem, load_sem,
):
    e = lax.axis_index("expert")
    f = lax.axis_index("fsdp")
    zh, x, c = e // 8, (e // 2) % 4, e % 2
    zl, y = f // 4, f % 4

    def z_peer(d):
        h = 1 - zh if d & 2 else zh
        l = 1 - zl if d & 1 else zl
        return (h * 8 + x * 2 + c, l * 4 + y)

    def xc(k, sign):
        dx, dc = k // 2, k % 2
        return lax.rem(x + (4 + sign * dx), 4), (1 - c if dc else c)

    def x_peer(k, sign):
        px, pc = xc(k, sign)
        return (zh * 8 + px * 2 + pc, f)

    def y_peer(j):
        return (e, zl * 4 + lax.rem(y + 4 + j, 4))

    def remote(src, dst, s, r, device):
        return pltpu.make_async_remote_copy(
            src_ref=src, dst_ref=dst, send_sem=s, recv_sem=r, device_id=device, device_id_type=MESH
        )

    barrier = pltpu.get_barrier_semaphore()
    peers = [z_peer(d) for d in (1, 2, 3)] + [x_peer(k, 1) for k in range(1, 8)] + [y_peer(j) for j in (1, 2, 3)]
    for peer in peers:
        pl.semaphore_signal(barrier, inc=1, device_id=peer, device_id_type=MESH)

    def columns(half, j):
        quarter = lax.rem(y + j, 4)
        return pl.ds(pl.multiple_of((half * 4 + quarter) * FEAT, 128), FEAT)

    own_rows = {
        j: pltpu.make_async_copy(grad.at[:, columns(zl, j)], raw.at[0, j], own_sem.at[j]) for j in ORDER
    }
    other_rows = {
        j: pltpu.make_async_copy(grad.at[:, columns(1 - zl, j)], merged.at[j], other_sem.at[j]) for j in ORDER
    }
    stash_copies = [pltpu.make_async_copy(scale_in.at[0, 0], scale, own_sem.at[5])]
    for s in range(16):
        sx, sc = xc(s % 8, -1)
        g = (1 - zh if s // 8 else zh) * 8 + sx * 2 + sc
        stash_copies.append(
            pltpu.make_async_copy(stash.at[0, 0, g], back.at[s // 8, pl.ds((s % 8) * CAP, CAP)], stash_sem.at[s])
        )
    own_weight = pltpu.make_async_copy(weight.at[0], wts.at[0], own_sem.at[4])
    for j in ORDER:
        own_rows[j].start()
        other_rows[j].start()

    expert_of = ids[...]
    same = lax.broadcasted_iota(jnp.int32, (16, ROWS), 0) == expert_of
    chosen = jnp.where(same, 1.0, 0.0)
    earlier = jnp.where(
        lax.broadcasted_iota(jnp.int32, (ROWS, ROWS), 0) < lax.broadcasted_iota(jnp.int32, (ROWS, ROWS), 1), 1.0, 0.0
    )
    count = jnp.dot(chosen.astype(BF), earlier.astype(BF), preferred_element_type=F32)
    slot = jnp.sum(chosen * count, axis=0, keepdims=True)
    key = expert_of * CAP + slot.astype(jnp.int32)
    keys[0] = jnp.broadcast_to(key, (8, ROWS))

    place = lax.broadcasted_iota(jnp.int32, (CAP, ROWS), 0)

    def make_pick(d):
        key_of = keys[d, 0:1, :]
        for k in range(8):
            px, pc = xc(k, 1)
            base = (zh * 8 + px * 2 + pc) * CAP
            pick[d, k * CAP : (k + 1) * CAP, :] = jnp.where(key_of - base == place, 1.0, 0.0).astype(BF)

    make_pick(0)
    near = jnp.broadcast_to(expert_of // 8 == zh, (8, ROWS)).astype(F32).T[:, 0:1] > 0.5

    raw_copies = {}
    for j in ORDER:
        raw_copies[1, j] = remote(merged.at[j], raw.at[1, j], raw_s.at[1, j], raw_r.at[1, j], z_peer(1))
        raw_copies[2, j] = remote(raw.at[1, j], raw.at[2, j], raw_s.at[2, j], raw_r.at[2, j], z_peer(3))
        raw_copies[3, j] = remote(
            grad.at[:, columns(1 - zl, j)], raw.at[3, j], raw_s.at[3, j], raw_r.at[3, j], z_peer(3)
        )

    loaded = []

    def own_ready(j):
        if j not in loaded:
            loaded.append(j)
            own_rows[j].wait()

    def merge(j):
        other_rows[j].wait()
        own_ready(j)

        def tile(t, _):
            at = pl.ds(pl.multiple_of(t * BLOCK, BLOCK), BLOCK)
            merged[j, :, at] = jnp.where(near, merged[j, :, at].astype(F32), raw[0, j, :, at].astype(F32)).astype(BF)
            return 0

        lax.fori_loop(0, FEAT // BLOCK, tile, 0)
    key_copies = [remote(keys.at[0], keys.at[d], key_s.at[d], key_r.at[d], z_peer(d)) for d in (1, 2, 3)]
    weight_copies = {j: remote(weight.at[0], wts.at[j], w_s.at[j], w_r.at[j], y_peer(-j)) for j in (1, 3)}
    upper, lower = pl.ds(0, FFW // 2), pl.ds(FFW // 2, FFW // 2)
    weight_copies[0] = remote(wts.at[1, upper], wts.at[2, upper], w_s.at[0], w_r.at[0], y_peer(-1))
    weight_copies[2] = remote(wts.at[3, lower], wts.at[2, lower], w_s.at[2], w_r.at[2], y_peer(1))
    hidden_copy = remote(hidden.at[:, pl.ds(0, SLOTS)], hidden.at[:, pl.ds(SLOTS, SLOTS)], hid_s.at[0], hid_r.at[0], z_peer(1))
    dh_copies = [remote(dh_out.at[zr], dh_in.at[zr], dh_s.at[zr], dh_r.at[zr], z_peer(1)) for zr in range(2)]
    far_copies = [
        remote(far_part.at[half], far_in.at[n], far_s.at[n], far_r.at[n], y_peer(1 - 2 * n))
        for n, half in enumerate((upper, lower))
    ]
    part_copies = {
        j: remote(wts.at[j], parts.at[j // 2], part_s.at[j // 2], part_r.at[j // 2], y_peer(j)) for j in (1, 3)
    }

    x_copies = {}
    order = []

    def put(d, j):
        unit = len(order)
        into = unit % OUTS
        if unit >= OUTS:
            for copy in x_copies[order[unit - OUTS]]:
                copy.wait_send()
        order.append((d, j))
        if d:
            raw_copies[d, j].wait_recv()
        else:
            own_ready(j)
        if d == 1:
            raw_copies[2, j].start()

        def tile(t, _):
            at = pl.ds(pl.multiple_of(t * 192, 192), 192)
            out[into, at, :] = jnp.dot(pick[d, at, :], raw[d, j], preferred_element_type=F32).astype(BF)
            return 0

        lax.fori_loop(0, 2, tile, 0)
        rows[j, PLACE[d], 0:CAP, :] = out[into, 0:CAP, :]

    def dispatch(d, j):
        if (d, j) not in order:
            put(d, j)
        unit = order.index((d, j))
        into = unit % OUTS
        x_copies[d, j] = []
        for k in range(1, 8):
            block = pl.ds(k * CAP, CAP)
            copy = remote(
                out.at[into, block, :], rows.at[j, PLACE[d], block, :], x_s.at[unit, k], x_r.at[unit, k], x_peer(k, 1)
            )
            copy.start()
            x_copies[d, j].append(copy)

    def gate_tile(s, _):
        zr, k = s // 8, s % 8
        dx, dc = k // 2, k % 2
        sx = lax.rem(x + 4 - dx, 4)
        sc = c + dc - 2 * c * dc
        sz = zh + zr - 2 * zh * zr
        factor = jnp.exp2(scale[sz * 8 + sx * 2 + sc].astype(F32)).T
        at = pl.ds(pl.multiple_of(k * CAP, CAP), CAP)
        for b in range(FFW // BLOCK):
            low, high = slice(b * BLOCK, (b + 1) * BLOCK), slice(FFW + b * BLOCK, FFW + (b + 1) * BLOCK)
            gate = back[zr, at, low].astype(F32) * factor[:, b : b + 1]
            up = back[zr, at, high].astype(F32) * factor[:, 8 + b : 9 + b]
            sig = 1.0 / (1.0 + jnp.exp(-gate))
            silu = gate * sig
            dh_out[zr, at, low] = (silu * up).astype(BF)
            coef[zr, at, low] = (up * sig * (1.0 + gate * (1.0 - sig))).astype(BF)
            coef[zr, at, high] = silu.astype(BF)
        return 0

    def turn(b, _):
        at = pl.ds(pl.multiple_of(b * BLOCK, BLOCK), BLOCK)
        for zr in range(2):
            hidden[at, zr * HALF : (zr + 1) * HALF] = dh_out[zr, :, at].T
        return 0

    def arrived(j, sources):
        for d in sources:
            for copy in x_copies[d, j]:
                copy.wait_recv()

    def d_hidden(d, j):
        arrived(j, (d,))

        def tile(n, _):
            at = pl.ds(pl.multiple_of(n * 256, 256), 256)
            dh[PLACE[d], :, at] += lax.dot_general(
                rows[j, PLACE[d]], wts[j, at, :], (((1,), (1,)), ((), ())), preferred_element_type=F32
            )
            return 0

        lax.fori_loop(0, FFW // 256, tile, 0)

    def d_hidden_all(j, start):
        def tile(n, _):
            at = pl.ds(pl.multiple_of(n * 256, 256), 256)
            term = lax.dot_general(
                rows[j].reshape(2 * SLOTS, FEAT), wts[j, at, :], (((1,), (1,)), ((), ())), preferred_element_type=F32
            ).reshape(4, HALF, 256)
            dh[:, :, at] = term if start else dh[:, :, at] + term
            return 0

        lax.fori_loop(0, FFW // 256, tile, 0)

    def partial(j):
        into = far_part if j == 2 else wts.at[j]
        for n in range(2):

            def tile(m, _, n=n):
                at = pl.ds(pl.multiple_of(n * (FFW // 2) + m * 256, 256), 256)
                term = jnp.dot(hidden[at, :], rows[j].reshape(2 * SLOTS, FEAT), preferred_element_type=F32)
                if j == 1 + 2 * n:
                    term += far_in[n, pl.ds(pl.multiple_of(m * 256, 256), 256), :].astype(F32)
                into[at, :] = term.astype(BF)
                return 0

            if j == 1 + 2 * n:
                far_copies[n].wait_recv()
            lax.fori_loop(0, 2, tile, 0)
            if j == 2:
                far_copies[n].start()
        if j in (1, 3):
            part_copies[j].start()

    def exchange(zr):
        dh_out[zr] = dh[PLACE[1 + 2 * zr]].astype(BF)
        dh_copies[zr].start()

    ret_copies, self_copies, fin_copies = {}, {}, []

    def send_back(zr):
        dh_copies[zr].wait_recv()
        for p in range(PARTS):
            cols = pl.ds(p * PCOLS, PCOLS)
            dh_cols = pl.ds((p * PCOLS) % FFW, PCOLS)

            def back_tile(k, _, cols=cols, dh_cols=dh_cols):
                at = pl.ds(pl.multiple_of(k * CAP, CAP), CAP)
                total = dh[PLACE[2 * zr], at, dh_cols] + dh_in[zr, at, dh_cols].astype(F32)
                back[zr, at, cols] = (total * coef[zr, at, cols].astype(F32)).astype(BF)
                return 0

            lax.fori_loop(0, 8, back_tile, 0)
            here = pltpu.make_async_copy(
                back.at[zr, pl.ds(0, CAP), cols], ret.at[zr, pl.ds(0, CAP), cols], self_sem.at[zr, p]
            )
            here.start()
            self_copies[zr, p] = here
            ret_copies[zr, p] = []
            for k in range(1, 8):
                block = pl.ds(k * CAP, CAP)
                copy = remote(
                    back.at[zr, block, cols], ret.at[zr, block, cols],
                    ret_s.at[zr, p, k], ret_r.at[zr, p, k], x_peer(k, -1),
                )
                copy.start()
                ret_copies[zr, p].append(copy)

    def collect(zr, p):
        cols = pl.ds(p * PCOLS, PCOLS)
        self_copies[zr, p].wait()
        for copy in ret_copies[zr, p]:
            copy.wait_recv()
        got = jnp.dot(pick_t[zr], ret[zr, :, cols], preferred_element_type=F32).astype(BF)
        if zr:
            fin[:, cols] = got
            copy = remote(fin.at[:, cols], far_grad.at[:, cols], fin_s.at[p], fin_r.at[p], z_peer(2))
            copy.start()
            fin_copies.append(copy)
        else:
            own_grad[:, cols] = got

    def collect_part(j):
        part_copies[j].wait_recv()
        part_copies[j].wait_send()
        load = pltpu.make_async_copy(parts.at[j // 2], wts.at[j], load_sem.at[j])
        load.start()
        return load

    a, b, g, o = ORDER
    put(0, a)
    pl.semaphore_wait(barrier, len(peers))
    dispatch(0, a)
    raw_copies[3, a].start()
    for copy in key_copies:
        copy.start()
    merge(a)
    raw_copies[1, a].start()
    weight_copies[1].start()
    weight_copies[3].start()
    merge(b)
    raw_copies[1, b].start()
    raw_copies[3, b].start()
    dispatch(0, b)
    dispatch(0, g)
    for copy in stash_copies:
        copy.start()
    merge(g)
    merge(o)
    own_weight.start()
    for copy in key_copies:
        copy.wait_recv()
    for d in (1, 3, 2):
        make_pick(d)
    for copy in stash_copies:
        copy.wait()
    lax.fori_loop(0, 16, gate_tile, 0)
    dispatch(1, a)
    dispatch(3, a)
    raw_copies[3, g].start()
    lax.fori_loop(0, FFW // BLOCK, turn, 0)
    hidden_copy.start()
    for n, d in enumerate((0, 2)):
        pick_t[n] = pick[d].astype(F32).T.astype(BF)
    dispatch(2, a)
    dispatch(1, b)
    dispatch(3, b)
    raw_copies[3, o].start()
    dispatch(2, b)
    raw_copies[1, g].start()
    weight_copies[1].wait_recv()
    weight_copies[0].start()
    weight_copies[3].wait_recv()
    weight_copies[2].start()
    dispatch(3, g)
    dispatch(3, o)
    raw_copies[1, o].start()
    arrived(a, (0, 1, 3, 2))
    hidden_copy.wait_recv()
    partial(a)
    dispatch(1, g)
    arrived(b, (0, 1, 3, 2))
    d_hidden_all(b, True)
    dispatch(2, g)
    weight_copies[0].wait_recv()
    weight_copies[2].wait_recv()
    dispatch(1, o)
    d_hidden_all(a, False)
    own_weight.wait()
    d_hidden(3, g)
    d_hidden(3, o)
    exchange(1)
    dispatch(2, o)
    dispatch(0, o)
    weight_copies[0].wait_send()
    partial(b)
    d_hidden(0, g)
    d_hidden(1, g)
    d_hidden(2, g)
    weight_copies[2].wait_send()
    partial(g)
    d_hidden(1, o)
    exchange(0)
    d_hidden(2, o)
    send_back(1)
    d_hidden(0, o)
    collect(1, 0)
    send_back(0)
    partial(o)
    for p in range(1, PARTS):
        collect(1, p)
    for p in range(PARTS - 1):
        collect(0, p)
    loads = [collect_part(b), collect_part(g)]
    for load in loads:
        load.wait()

    def sum_tile(t, _):
        at = pl.ds(pl.multiple_of(t * 64, 64), 64)
        total = wts[0, at, :].astype(F32)
        for j in (1, 3):
            total += wts[j, at, :].astype(F32)
        weight_grad[0, at, :] = total.astype(BF)
        return 0

    lax.fori_loop(0, FFW // 64, sum_tile, 0)
    collect(0, PARTS - 1)
    for copy in fin_copies:
        copy.wait_recv()
    sent = list(raw_copies.values()) + key_copies + [weight_copies[1], weight_copies[3]] + [hidden_copy] + dh_copies
    sent += fin_copies + far_copies
    for unit in order[len(order) - OUTS :]:
        sent += x_copies[unit]
    for copies in ret_copies.values():
        sent += copies
    for copy in sent:
        copy.wait_send()


def last(own, far, share, in_grad, weight_grad, total, sems):
    rows = ROWS // 4
    out = pltpu.make_async_copy(share, weight_grad, sems.at[4])
    out.start()
    stores = []
    for t in range(4):
        at = pl.ds(t * rows, rows)
        total[at, :] = own[at, :] + far[at, :]
        store = pltpu.make_async_copy(total.at[at], in_grad.at[at], sems.at[t])
        store.start()
        stores.append(store)
    for store in stores:
        store.wait()
    out.wait()


def finish(own_grad, far_grad, weight_grad):
    hbm = pl.BlockSpec(memory_space=pl.ANY)
    vmem = pl.BlockSpec(memory_space=pltpu.VMEM)
    return pl.pallas_call(
        last,
        out_shape=(
            jax.ShapeDtypeStruct(own_grad.shape, BF),
            jax.ShapeDtypeStruct(weight_grad.shape, BF),
        ),
        in_specs=[vmem, vmem, vmem],
        out_specs=(hbm, hbm),
        scratch_shapes=[
            pltpu.VMEM((ROWS, 2 * FFW), BF),
            pltpu.SemaphoreType.DMA((5,)),
        ],
        compiler_params=pltpu.CompilerParams(vmem_limit_bytes=8 * 2**20),
        name="finish",
    )(own_grad, far_grad, weight_grad)


def shards(out_grad, expert_ids, stash_codes, stash_scale, down_weight):
    dma = pltpu.SemaphoreType.DMA
    hbm = pl.BlockSpec(memory_space=pl.ANY)
    vmem = pl.BlockSpec(memory_space=pltpu.VMEM)
    scratch = [
        pltpu.VMEM((4, 4, ROWS, FEAT), BF),
        pltpu.VMEM((4, ROWS, FEAT), BF),
        pltpu.VMEM((OUTS, HALF, FEAT), BF),
        pltpu.VMEM((4, 4, HALF, FEAT), BF),
        pltpu.VMEM((4, FFW, FEAT), BF),
        pltpu.VMEM((FFW, FEAT), BF),
        pltpu.VMEM((2, FFW // 2, FEAT), BF),
        pltpu.VMEM((FFW, 2 * SLOTS), BF),
        pltpu.VMEM((2, HALF, 2 * FFW), BF),
        pltpu.VMEM((4, HALF, FFW), F32),
        pltpu.VMEM((2, HALF, FFW), BF),
        pltpu.VMEM((2, HALF, FFW), BF),
        pltpu.VMEM((2, HALF, 2 * FFW), BF),
        pltpu.VMEM((2, HALF, 2 * FFW), BF),
        pltpu.VMEM((4, HALF, ROWS), BF),
        pltpu.VMEM((2, ROWS, HALF), BF),
        pltpu.VMEM((4, 8, ROWS), jnp.int32),
        pltpu.VMEM((ROWS, 2 * FFW), BF),
        pltpu.VMEM((16, 16, CAP), jnp.int32),
    ]
    for shape in [(4, 4), (4,), (4,), (16, 8), (1,), (2,), (2,), (2,), (2, PARTS, 8), (PARTS,)]:
        scratch += [dma(shape), dma(shape)]
    scratch += [dma((6,)), dma((4,)), dma((16,)), dma((2, PARTS)), dma((4,))]
    own_grad, far_grad, weight_grad, _ = pl.pallas_call(
        kernel,
        out_shape=(
            pltpu.VMEM((ROWS, 2 * FFW), BF),
            pltpu.VMEM((ROWS, 2 * FFW), BF),
            pltpu.VMEM((1, FFW, FEAT), BF),
            jax.ShapeDtypeStruct((2, FFW, FEAT), BF),
        ),
        in_specs=[hbm, vmem, hbm, hbm, hbm],
        out_specs=(vmem, vmem, vmem, hbm),
        scratch_shapes=scratch,
        compiler_params=pltpu.CompilerParams(
            collective_id=0, has_side_effects=True, vmem_limit_bytes=58 * 2**20
        ),
        name="expert_backward",
    )(out_grad, expert_ids.reshape(1, ROWS), stash_codes, jnp.swapaxes(stash_scale, 3, 4), down_weight)
    return finish(own_grad, far_grad, weight_grad)


def solution(mesh):
    placed = (
        P(("expert", "fsdp"), None),
        P(("expert", "fsdp"), None),
        P("expert", "fsdp", None, None, None),
        P("expert", "fsdp", None, None, None),
        P("expert", None, "fsdp"),
    )
    return jax.shard_map(
        shards,
        mesh=mesh,
        in_specs=placed,
        out_specs=(P(("expert", "fsdp"), None), P("expert", None, "fsdp")),
        check_vma=False,
    )
```

```python
import jax
import jax.numpy as jnp
from jax import lax
from jax.experimental import pallas as pl
from jax.experimental.pallas import tpu as pltpu
from jax.sharding import PartitionSpec as P

FFW = 1024
BLOCK = 128
CAP = 48
ROWS = 256
FEAT = 896
HALF = 8 * CAP
SLOTS = 2 * HALF
OUTS = 6
PLACE = (0, 2, 1, 3)
ORDER = (2, 1, 3, 0)
PARTS = 4
PCOLS = 2 * FFW // PARTS
MESH = pl.DeviceIdType.MESH
BF = jnp.bfloat16
F32 = jnp.float32


def kernel(
    grad, ids, stash, scale_in, weight,
    own_grad, far_grad, weight_grad, parts,
    raw, merged, out, rows, wts, far_part, far_in, hidden, coef, dh, dh_out, dh_in, back, ret, pick, pick_t, keys, fin, scale,
    raw_s, raw_r, key_s, key_r, w_s, w_r, x_s, x_r, hid_s, hid_r, dh_s, dh_r, far_s, far_r, part_s, part_r, ret_s, ret_r, fin_s, fin_r,
    own_sem, other_sem, stash_sem, self_sem, load_sem,
):
    e = lax.axis_index("expert")
    f = lax.axis_index("fsdp")
    zh, x, c = e // 8, (e // 2) % 4, e % 2
    zl, y = f // 4, f % 4

    def z_peer(d):
        h = 1 - zh if d & 2 else zh
        l = 1 - zl if d & 1 else zl
        return (h * 8 + x * 2 + c, l * 4 + y)

    def xc(k, sign):
        dx, dc = k // 2, k % 2
        return lax.rem(x + (4 + sign * dx), 4), (1 - c if dc else c)

    def x_peer(k, sign):
        px, pc = xc(k, sign)
        return (zh * 8 + px * 2 + pc, f)

    def y_peer(j):
        return (e, zl * 4 + lax.rem(y + 4 + j, 4))

    def remote(src, dst, s, r, device):
        return pltpu.make_async_remote_copy(
            src_ref=src, dst_ref=dst, send_sem=s, recv_sem=r, device_id=device, device_id_type=MESH
        )

    barrier = pltpu.get_barrier_semaphore()
    peers = [z_peer(d) for d in (1, 2, 3)] + [x_peer(k, 1) for k in range(1, 8)] + [y_peer(j) for j in (1, 2, 3)]
    for peer in peers:
        pl.semaphore_signal(barrier, inc=1, device_id=peer, device_id_type=MESH)

    def columns(half, j):
        quarter = lax.rem(y + j, 4)
        return pl.ds(pl.multiple_of((half * 4 + quarter) * FEAT, 128), FEAT)

    own_rows = {
        j: pltpu.make_async_copy(grad.at[:, columns(zl, j)], raw.at[0, j], own_sem.at[j]) for j in ORDER
    }
    other_rows = {
        j: pltpu.make_async_copy(grad.at[:, columns(1 - zl, j)], merged.at[j], other_sem.at[j]) for j in ORDER
    }
    stash_copies = [pltpu.make_async_copy(scale_in.at[0, 0], scale, own_sem.at[5])]
    for s in range(16):
        sx, sc = xc(s % 8, -1)
        g = (1 - zh if s // 8 else zh) * 8 + sx * 2 + sc
        stash_copies.append(
            pltpu.make_async_copy(stash.at[0, 0, g], back.at[s // 8, pl.ds((s % 8) * CAP, CAP)], stash_sem.at[s])
        )
    own_weight = pltpu.make_async_copy(weight.at[0], wts.at[0], own_sem.at[4])
    for j in ORDER:
        own_rows[j].start()
        other_rows[j].start()

    expert_of = ids[...]
    same = lax.broadcasted_iota(jnp.int32, (16, ROWS), 0) == expert_of
    chosen = jnp.where(same, 1.0, 0.0)
    earlier = jnp.where(
        lax.broadcasted_iota(jnp.int32, (ROWS, ROWS), 0) < lax.broadcasted_iota(jnp.int32, (ROWS, ROWS), 1), 1.0, 0.0
    )
    count = jnp.dot(chosen.astype(BF), earlier.astype(BF), preferred_element_type=F32)
    slot = jnp.sum(chosen * count, axis=0, keepdims=True)
    key = expert_of * CAP + slot.astype(jnp.int32)
    keys[0] = jnp.broadcast_to(key, (8, ROWS))

    place = lax.broadcasted_iota(jnp.int32, (CAP, ROWS), 0)

    def make_pick(d):
        key_of = keys[d, 0:1, :]
        for k in range(8):
            px, pc = xc(k, 1)
            base = (zh * 8 + px * 2 + pc) * CAP
            pick[d, k * CAP : (k + 1) * CAP, :] = jnp.where(key_of - base == place, 1.0, 0.0).astype(BF)

    make_pick(0)
    near = jnp.broadcast_to(expert_of // 8 == zh, (8, ROWS)).astype(F32).T[:, 0:1] > 0.5

    raw_copies = {}
    for j in ORDER:
        raw_copies[1, j] = remote(merged.at[j], raw.at[1, j], raw_s.at[1, j], raw_r.at[1, j], z_peer(1))
        raw_copies[2, j] = remote(raw.at[1, j], raw.at[2, j], raw_s.at[2, j], raw_r.at[2, j], z_peer(3))
        raw_copies[3, j] = remote(
            grad.at[:, columns(1 - zl, j)], raw.at[3, j], raw_s.at[3, j], raw_r.at[3, j], z_peer(3)
        )

    loaded = []

    def own_ready(j):
        if j not in loaded:
            loaded.append(j)
            own_rows[j].wait()

    def merge(j):
        other_rows[j].wait()
        own_ready(j)

        def tile(t, _):
            at = pl.ds(pl.multiple_of(t * BLOCK, BLOCK), BLOCK)
            merged[j, :, at] = jnp.where(near, merged[j, :, at].astype(F32), raw[0, j, :, at].astype(F32)).astype(BF)
            return 0

        lax.fori_loop(0, FEAT // BLOCK, tile, 0)
    key_copies = [remote(keys.at[0], keys.at[d], key_s.at[d], key_r.at[d], z_peer(d)) for d in (1, 2, 3)]
    weight_copies = {j: remote(weight.at[0], wts.at[j], w_s.at[j], w_r.at[j], y_peer(-j)) for j in (1, 3)}
    upper, lower = pl.ds(0, FFW // 2), pl.ds(FFW // 2, FFW // 2)
    weight_copies[0] = remote(wts.at[1, upper], wts.at[2, upper], w_s.at[0], w_r.at[0], y_peer(-1))
    weight_copies[2] = remote(wts.at[3, lower], wts.at[2, lower], w_s.at[2], w_r.at[2], y_peer(1))
    hidden_copy = remote(hidden.at[:, pl.ds(0, SLOTS)], hidden.at[:, pl.ds(SLOTS, SLOTS)], hid_s.at[0], hid_r.at[0], z_peer(1))
    dh_copies = [remote(dh_out.at[zr], dh_in.at[zr], dh_s.at[zr], dh_r.at[zr], z_peer(1)) for zr in range(2)]
    far_copies = [
        remote(far_part.at[half], far_in.at[n], far_s.at[n], far_r.at[n], y_peer(1 - 2 * n))
        for n, half in enumerate((upper, lower))
    ]
    part_copies = {
        j: remote(wts.at[j], parts.at[j // 2], part_s.at[j // 2], part_r.at[j // 2], y_peer(j)) for j in (1, 3)
    }

    x_copies = {}
    order = []

    def put(d, j):
        unit = len(order)
        into = unit % OUTS
        if unit >= OUTS:
            for copy in x_copies[order[unit - OUTS]]:
                copy.wait_send()
        order.append((d, j))
        if d:
            raw_copies[d, j].wait_recv()
        else:
            own_ready(j)
        if d == 1:
            raw_copies[2, j].start()

        def tile(t, _):
            at = pl.ds(pl.multiple_of(t * 192, 192), 192)
            out[into, at, :] = jnp.dot(pick[d, at, :], raw[d, j], preferred_element_type=F32).astype(BF)
            return 0

        lax.fori_loop(0, 2, tile, 0)
        rows[j, PLACE[d], 0:CAP, :] = out[into, 0:CAP, :]

    def dispatch(d, j):
        if (d, j) not in order:
            put(d, j)
        unit = order.index((d, j))
        into = unit % OUTS
        x_copies[d, j] = []
        for k in range(1, 8):
            block = pl.ds(k * CAP, CAP)
            copy = remote(
                out.at[into, block, :], rows.at[j, PLACE[d], block, :], x_s.at[unit, k], x_r.at[unit, k], x_peer(k, 1)
            )
            copy.start()
            x_copies[d, j].append(copy)

    def gate_tile(s, _):
        zr, k = s // 8, s % 8
        dx, dc = k // 2, k % 2
        sx = lax.rem(x + 4 - dx, 4)
        sc = c + dc - 2 * c * dc
        sz = zh + zr - 2 * zh * zr
        factor = jnp.exp2(scale[sz * 8 + sx * 2 + sc].astype(F32)).T
        at = pl.ds(pl.multiple_of(k * CAP, CAP), CAP)
        for b in range(FFW // BLOCK):
            low, high = slice(b * BLOCK, (b + 1) * BLOCK), slice(FFW + b * BLOCK, FFW + (b + 1) * BLOCK)
            gate = back[zr, at, low].astype(F32) * factor[:, b : b + 1]
            up = back[zr, at, high].astype(F32) * factor[:, 8 + b : 9 + b]
            sig = 1.0 / (1.0 + jnp.exp(-gate))
            silu = gate * sig
            dh_out[zr, at, low] = (silu * up).astype(BF)
            coef[zr, at, low] = (up * sig * (1.0 + gate * (1.0 - sig))).astype(BF)
            coef[zr, at, high] = silu.astype(BF)
        return 0

    def turn(b, _):
        at = pl.ds(pl.multiple_of(b * BLOCK, BLOCK), BLOCK)
        for zr in range(2):
            hidden[at, zr * HALF : (zr + 1) * HALF] = dh_out[zr, :, at].T
        return 0

    def arrived(j, sources):
        for d in sources:
            for copy in x_copies[d, j]:
                copy.wait_recv()

    def d_hidden(d, j):
        arrived(j, (d,))

        def tile(n, _):
            at = pl.ds(pl.multiple_of(n * 256, 256), 256)
            dh[PLACE[d], :, at] += lax.dot_general(
                rows[j, PLACE[d]], wts[j, at, :], (((1,), (1,)), ((), ())), preferred_element_type=F32
            )
            return 0

        lax.fori_loop(0, FFW // 256, tile, 0)

    def d_hidden_all(j, start):
        def tile(n, _):
            at = pl.ds(pl.multiple_of(n * 256, 256), 256)
            term = lax.dot_general(
                rows[j].reshape(2 * SLOTS, FEAT), wts[j, at, :], (((1,), (1,)), ((), ())), preferred_element_type=F32
            ).reshape(4, HALF, 256)
            dh[:, :, at] = term if start else dh[:, :, at] + term
            return 0

        lax.fori_loop(0, FFW // 256, tile, 0)

    def partial(j):
        into = far_part if j == 2 else wts.at[j]
        for n in range(2):

            def tile(m, _, n=n):
                at = pl.ds(pl.multiple_of(n * (FFW // 2) + m * 256, 256), 256)
                term = jnp.dot(hidden[at, :], rows[j].reshape(2 * SLOTS, FEAT), preferred_element_type=F32)
                if j == 1 + 2 * n:
                    term += far_in[n, pl.ds(pl.multiple_of(m * 256, 256), 256), :].astype(F32)
                into[at, :] = term.astype(BF)
                return 0

            if j == 1 + 2 * n:
                far_copies[n].wait_recv()
            lax.fori_loop(0, 2, tile, 0)
            if j == 2:
                far_copies[n].start()
        if j in (1, 3):
            part_copies[j].start()

    def exchange(zr):
        dh_out[zr] = dh[PLACE[1 + 2 * zr]].astype(BF)
        dh_copies[zr].start()

    ret_copies, self_copies, fin_copies = {}, {}, []

    def send_back(zr):
        dh_copies[zr].wait_recv()
        for p in range(PARTS):
            cols = pl.ds(p * PCOLS, PCOLS)
            dh_cols = pl.ds((p * PCOLS) % FFW, PCOLS)

            def back_tile(k, _, cols=cols, dh_cols=dh_cols):
                at = pl.ds(pl.multiple_of(k * CAP, CAP), CAP)
                total = dh[PLACE[2 * zr], at, dh_cols] + dh_in[zr, at, dh_cols].astype(F32)
                back[zr, at, cols] = (total * coef[zr, at, cols].astype(F32)).astype(BF)
                return 0

            lax.fori_loop(0, 8, back_tile, 0)
            here = pltpu.make_async_copy(
                back.at[zr, pl.ds(0, CAP), cols], ret.at[zr, pl.ds(0, CAP), cols], self_sem.at[zr, p]
            )
            here.start()
            self_copies[zr, p] = here
            ret_copies[zr, p] = []
            for k in range(1, 8):
                block = pl.ds(k * CAP, CAP)
                copy = remote(
                    back.at[zr, block, cols], ret.at[zr, block, cols],
                    ret_s.at[zr, p, k], ret_r.at[zr, p, k], x_peer(k, -1),
                )
                copy.start()
                ret_copies[zr, p].append(copy)

    def collect(zr, p):
        cols = pl.ds(p * PCOLS, PCOLS)
        self_copies[zr, p].wait()
        for copy in ret_copies[zr, p]:
            copy.wait_recv()
        got = jnp.dot(pick_t[zr], ret[zr, :, cols], preferred_element_type=F32).astype(BF)
        if zr:
            fin[:, cols] = got
            copy = remote(fin.at[:, cols], far_grad.at[:, cols], fin_s.at[p], fin_r.at[p], z_peer(2))
            copy.start()
            fin_copies.append(copy)
        else:
            own_grad[:, cols] = got

    def collect_part(j):
        part_copies[j].wait_recv()
        part_copies[j].wait_send()
        load = pltpu.make_async_copy(parts.at[j // 2], wts.at[j], load_sem.at[j])
        load.start()
        return load

    a, b, g, o = ORDER
    put(0, a)
    pl.semaphore_wait(barrier, len(peers))
    dispatch(0, a)
    raw_copies[3, a].start()
    for copy in key_copies:
        copy.start()
    merge(a)
    raw_copies[1, a].start()
    weight_copies[1].start()
    weight_copies[3].start()
    merge(b)
    raw_copies[1, b].start()
    raw_copies[3, b].start()
    dispatch(0, b)
    dispatch(0, g)
    for copy in stash_copies:
        copy.start()
    merge(g)
    merge(o)
    own_weight.start()
    for copy in key_copies:
        copy.wait_recv()
    for d in (1, 3, 2):
        make_pick(d)
    for copy in stash_copies:
        copy.wait()
    lax.fori_loop(0, 16, gate_tile, 0)
    dispatch(1, a)
    dispatch(3, a)
    raw_copies[3, g].start()
    lax.fori_loop(0, FFW // BLOCK, turn, 0)
    hidden_copy.start()
    for n, d in enumerate((0, 2)):
        pick_t[n] = pick[d].astype(F32).T.astype(BF)
    dispatch(2, a)
    dispatch(1, b)
    dispatch(3, b)
    raw_copies[3, o].start()
    dispatch(2, b)
    raw_copies[1, g].start()
    weight_copies[1].wait_recv()
    weight_copies[0].start()
    weight_copies[3].wait_recv()
    weight_copies[2].start()
    dispatch(3, g)
    dispatch(3, o)
    raw_copies[1, o].start()
    arrived(a, (0, 1, 3, 2))
    dispatch(1, g)
    hidden_copy.wait_recv()
    partial(a)
    arrived(b, (0, 1, 3, 2))
    d_hidden_all(b, True)
    dispatch(2, g)
    weight_copies[0].wait_recv()
    weight_copies[2].wait_recv()
    dispatch(1, o)
    d_hidden_all(a, False)
    own_weight.wait()
    d_hidden(3, g)
    d_hidden(3, o)
    exchange(1)
    dispatch(2, o)
    dispatch(0, o)
    weight_copies[0].wait_send()
    partial(b)
    d_hidden(0, g)
    d_hidden(1, g)
    d_hidden(2, g)
    weight_copies[2].wait_send()
    partial(g)
    d_hidden(1, o)
    exchange(0)
    d_hidden(2, o)
    send_back(1)
    d_hidden(0, o)
    collect(1, 0)
    send_back(0)
    partial(o)
    for p in range(1, PARTS):
        collect(1, p)
    for p in range(PARTS - 1):
        collect(0, p)
    loads = [collect_part(b), collect_part(g)]
    for load in loads:
        load.wait()

    def sum_tile(t, _):
        at = pl.ds(pl.multiple_of(t * 64, 64), 64)
        total = wts[0, at, :].astype(F32)
        for j in (1, 3):
            total += wts[j, at, :].astype(F32)
        weight_grad[0, at, :] = total.astype(BF)
        return 0

    lax.fori_loop(0, FFW // 64, sum_tile, 0)
    collect(0, PARTS - 1)
    for copy in fin_copies:
        copy.wait_recv()
    sent = list(raw_copies.values()) + key_copies + [weight_copies[1], weight_copies[3]] + [hidden_copy] + dh_copies
    sent += fin_copies + far_copies
    for unit in order[len(order) - OUTS :]:
        sent += x_copies[unit]
    for copies in ret_copies.values():
        sent += copies
    for copy in sent:
        copy.wait_send()


def last(own, far, share, in_grad, weight_grad, total, sems):
    rows = ROWS // 4
    out = pltpu.make_async_copy(share, weight_grad, sems.at[4])
    out.start()
    stores = []
    for t in range(4):
        at = pl.ds(t * rows, rows)
        total[at, :] = own[at, :] + far[at, :]
        store = pltpu.make_async_copy(total.at[at], in_grad.at[at], sems.at[t])
        store.start()
        stores.append(store)
    for store in stores:
        store.wait()
    out.wait()


def finish(own_grad, far_grad, weight_grad):
    hbm = pl.BlockSpec(memory_space=pl.ANY)
    vmem = pl.BlockSpec(memory_space=pltpu.VMEM)
    return pl.pallas_call(
        last,
        out_shape=(
            jax.ShapeDtypeStruct(own_grad.shape, BF),
            jax.ShapeDtypeStruct(weight_grad.shape, BF),
        ),
        in_specs=[vmem, vmem, vmem],
        out_specs=(hbm, hbm),
        scratch_shapes=[
            pltpu.VMEM((ROWS, 2 * FFW), BF),
            pltpu.SemaphoreType.DMA((5,)),
        ],
        compiler_params=pltpu.CompilerParams(vmem_limit_bytes=8 * 2**20),
        name="finish",
    )(own_grad, far_grad, weight_grad)


def shards(out_grad, expert_ids, stash_codes, stash_scale, down_weight):
    dma = pltpu.SemaphoreType.DMA
    hbm = pl.BlockSpec(memory_space=pl.ANY)
    vmem = pl.BlockSpec(memory_space=pltpu.VMEM)
    scratch = [
        pltpu.VMEM((4, 4, ROWS, FEAT), BF),
        pltpu.VMEM((4, ROWS, FEAT), BF),
        pltpu.VMEM((OUTS, HALF, FEAT), BF),
        pltpu.VMEM((4, 4, HALF, FEAT), BF),
        pltpu.VMEM((4, FFW, FEAT), BF),
        pltpu.VMEM((FFW, FEAT), BF),
        pltpu.VMEM((2, FFW // 2, FEAT), BF),
        pltpu.VMEM((FFW, 2 * SLOTS), BF),
        pltpu.VMEM((2, HALF, 2 * FFW), BF),
        pltpu.VMEM((4, HALF, FFW), F32),
        pltpu.VMEM((2, HALF, FFW), BF),
        pltpu.VMEM((2, HALF, FFW), BF),
        pltpu.VMEM((2, HALF, 2 * FFW), BF),
        pltpu.VMEM((2, HALF, 2 * FFW), BF),
        pltpu.VMEM((4, HALF, ROWS), BF),
        pltpu.VMEM((2, ROWS, HALF), BF),
        pltpu.VMEM((4, 8, ROWS), jnp.int32),
        pltpu.VMEM((ROWS, 2 * FFW), BF),
        pltpu.VMEM((16, 16, CAP), jnp.int32),
    ]
    for shape in [(4, 4), (4,), (4,), (16, 8), (1,), (2,), (2,), (2,), (2, PARTS, 8), (PARTS,)]:
        scratch += [dma(shape), dma(shape)]
    scratch += [dma((6,)), dma((4,)), dma((16,)), dma((2, PARTS)), dma((4,))]
    own_grad, far_grad, weight_grad, _ = pl.pallas_call(
        kernel,
        out_shape=(
            pltpu.VMEM((ROWS, 2 * FFW), BF),
            pltpu.VMEM((ROWS, 2 * FFW), BF),
            pltpu.VMEM((1, FFW, FEAT), BF),
            jax.ShapeDtypeStruct((2, FFW, FEAT), BF),
        ),
        in_specs=[hbm, vmem, hbm, hbm, hbm],
        out_specs=(vmem, vmem, vmem, hbm),
        scratch_shapes=scratch,
        compiler_params=pltpu.CompilerParams(
            collective_id=0, has_side_effects=True, vmem_limit_bytes=58 * 2**20
        ),
        name="expert_backward",
    )(out_grad, expert_ids.reshape(1, ROWS), stash_codes, jnp.swapaxes(stash_scale, 3, 4), down_weight)
    return finish(own_grad, far_grad, weight_grad)


def solution(mesh):
    placed = (
        P(("expert", "fsdp"), None),
        P(("expert", "fsdp"), None),
        P("expert", "fsdp", None, None, None),
        P("expert", "fsdp", None, None, None),
        P("expert", None, "fsdp"),
    )
    return jax.shard_map(
        shards,
        mesh=mesh,
        in_specs=placed,
        out_specs=(P(("expert", "fsdp"), None), P("expert", None, "fsdp")),
        check_vma=False,
    )
```
